256 devices in a mesh: ctx: 16 (over z, x_lo), tp: 8 (over y, core), rep: 2 (over x_hi).
Axes of the slice: x: 4 (x_hi: 2, x_lo: 2; x = x_hi * 2 + x_lo), y: 4, z: 8, core: 2. Of those that a mesh axis runs over, the one named last changes fastest.
Arguments:
- queries: bfloat16 [2048, 8192], P(('rep', 'ctx'), 'tp'), parts along dimension 0, may hold values from -12 to 12
- new_keys: bfloat16 [2048, 1024], P(('rep', 'ctx'), 'tp'), parts along dimension 0, may hold values from -4 to 4
- new_values: bfloat16 [2048, 1024], P(('rep', 'ctx'), 'tp'), parts along dimension 0, may hold values from -4 to 4
- cache_keys: bfloat16 [131072, 1024], P(('rep', 'ctx'), 'tp'), parts along dimension 0, may hold values from -4 to 4
- cache_values: bfloat16 [131072, 1024], P(('rep', 'ctx'), 'tp'), parts along dimension 0, may hold values from -4 to 4
- block_owner: int32 [512], P(('rep', 'ctx')), parts along dimension 0, may hold values from 0 to 255, as said below
- history_len: int32 [4], P('rep'), parts along dimension 0, may hold values from 8192 to 32768, as said below
Outputs:
- attended: float32 [2048, 8192], P(('rep', 'ctx'), 'tp'), parts along dimension 0
The draws below stay inside these ranges and needn't reach their ends.
There are 2 independent parts, one for each index of `rep`. The reference program is written for one: setup_inputs(seed, part) draws one part's arguments, and reference() takes and returns one part's arrays. A program takes and returns all parts, laid end to end along the dimension named above; each array names one. Nothing has to cross between parts.
Inputs may be any that keep to these rules, and one draw needn't show every extreme that they name: block_owner is a permutation of 0 to 255; logical block b of request r lies on ctx index (b + o_r) mod 16 for an offset o_r of the request. `history_len`: one request has a full history.
All inputs are finite; a program needn't handle non-finite values.
Results may differ from the reference program's by a relative error of at most 0.009.
Values may be sent and summed in bfloat16 or wider, within the bound.
A program may use at most 64 MiB of HBM per device.

```python
import math
import jax
import jax.numpy as jnp
from jax import lax

QH = 64
KVH = 8
HD = 128
REQS = 2
BLOCK = 256
BLK_DEV = 16
NEW = 1024
NB = 256
CAPB = 128
CACHE = 65536


def block_layout(key):
    key = jax.random.fold_in(key, 101)
    devices = NB // BLK_DEV
    offsets = jax.random.randint(jax.random.fold_in(key, 1), (REQS,), 0, devices)
    perms = jax.vmap(lambda k: jax.random.permutation(k, BLK_DEV))(jax.random.split(jax.random.fold_in(key, 2), devices))
    logical = jnp.arange(NB, dtype=jnp.int32)
    request = logical // CAPB
    within_req = logical % CAPB
    device = (within_req + offsets[request]) % devices
    slot = request * (BLK_DEV // REQS) + within_req // devices
    return device * BLK_DEV + perms[device, slot]


def draw_block_owner(key, part):
    phys = block_layout(key)
    return jnp.zeros((NB,), jnp.int32).at[phys].set(jnp.arange(NB, dtype=jnp.int32))


def draw_history_len(key, part):
    key = jax.random.fold_in(key, 5)
    full_len = CAPB * BLOCK
    lens = jax.random.randint(jax.random.fold_in(key, 1), (REQS,), full_len // 4, full_len + 1)
    which = jax.random.randint(jax.random.fold_in(key, 2), (), 0, REQS)
    return jnp.where(jnp.arange(REQS) == which, full_len, lens).astype(jnp.int32)


def draw_queries(key, part):
    key = jax.random.fold_in(key, 7)
    base = jnp.clip(jax.random.normal(key, (NEW, QH * HD), jnp.float32), -4.0, 4.0)
    return base.astype(jnp.bfloat16)


def draw_cache_keys(key, part):
    key = jax.random.fold_in(key, 9)
    base = jnp.clip(jax.random.normal(key, (CACHE, KVH * HD), jnp.float32), -4.0, 4.0)
    return base.astype(jnp.bfloat16)


def steps_of(key, dims, cuts, least, high):
    def one(dim, blocks):
        heights = jax.random.uniform(jax.random.fold_in(jax.random.fold_in(key, 6), dim), (blocks,), jnp.float32, least / len(cuts), high / len(cuts))
        return jnp.repeat(jnp.exp(heights), dims[dim] // blocks).reshape((-1,) + (1,) * (len(dims) - dim - 1))

    gain = one(*cuts[0])
    for cut in cuts[1:]:
        gain = gain * one(*cut)
    return gain


def noise(own_key, shape, width, reach, cuts=(), kind=jnp.bfloat16):
    array = jax.random.normal(own_key, shape, jnp.float32) * width
    if len(cuts) > 0:
        array = steps_of(own_key, shape, cuts, -0.22, 0.18) * array
    return jnp.clip(array, min=-reach, max=reach).astype(kind)


def setup_inputs(seed: int = 0, part: int = 0) -> dict:
    splits = jax.random.split(jax.random.key(seed), 8)
    part_keys = jax.random.split(jax.random.fold_in(splits[7], part), 8)
    queries = draw_queries(jax.random.fold_in(jax.random.fold_in(splits[7], part), 71), part)
    new_keys = noise(part_keys[1], (NEW, KVH * HD), 1.0, 4.0, ((0, 16), (1, 8)))
    new_values = noise(part_keys[2], (NEW, KVH * HD), 1.0, 4.0, ((0, 16), (1, 8)))
    cache_keys = draw_cache_keys(jax.random.fold_in(jax.random.fold_in(splits[7], part), 71), part)
    cache_values = noise(part_keys[4], (CACHE, KVH * HD), 1.0, 4.0, ((0, 16), (1, 8)))
    block_owner = draw_block_owner(jax.random.fold_in(jax.random.fold_in(splits[7], part), 71), part)
    history_len = draw_history_len(jax.random.fold_in(jax.random.fold_in(splits[7], part), 71), part)
    return {"queries": queries, "new_keys": new_keys, "new_values": new_values, "cache_keys": cache_keys, "cache_values": cache_values, "block_owner": block_owner, "history_len": history_len}


def reference(queries, new_keys, new_values, cache_keys, cache_values, block_owner, history_len):
    tok = NEW // REQS
    grp = QH // KVH
    span = CAPB * BLOCK
    scale = 1.0 / math.sqrt(HD)
    order = jnp.argsort(block_owner).astype(jnp.int32)

    def logical(cache):
        return cache.reshape(NB, BLOCK, KVH * HD)[order].reshape(REQS, span, KVH, HD)
    cached_k = logical(cache_keys)
    cached_v = logical(cache_values)
    q_all = queries.reshape(REQS, tok, KVH, grp, HD)
    fresh_k = new_keys.reshape(REQS, tok, KVH, HD)
    fresh_v = new_values.reshape(REQS, tok, KVH, HD)
    qblk = math.gcd(tok, 64)
    key_index = jnp.arange(span + tok, dtype=jnp.int32)
    results = []
    for req in range(REQS):
        keys = jnp.concatenate([cached_k[req], fresh_k[req]], 0).transpose(1, 0, 2)
        vals = jnp.concatenate([cached_v[req], fresh_v[req]], 0).transpose(1, 0, 2)
        q_req = q_all[req].transpose(1, 0, 2, 3).reshape(KVH, tok // qblk, qblk, grp, HD)
        limit = history_len[req]

        def per_head(item):
            q_head, k_head, v_head = item
            k_float = k_head.astype(jnp.float32)
            v_float = v_head.astype(jnp.float32)

            def per_block(arg):
                q_blk, start = arg
                s = jnp.einsum('qjd,kd->qjk', q_blk.astype(jnp.float32), k_float) * scale
                q_index = start + jnp.arange(qblk, dtype=jnp.int32)
                mask = jnp.where(key_index[None, :] < span, key_index[None, :] < limit, key_index[None, :] - span <= q_index[:, None])
                wide = mask[:, None, :]
                top = lax.optimization_barrier(jnp.max(jnp.where(wide, s, -1e+30), -1, keepdims=True))
                probs = jnp.where(wide, jnp.exp(s - top), 0.0)
                total = lax.optimization_barrier(jnp.sum(probs, -1, keepdims=True))
                rounded = lax.optimization_barrier(probs.astype(jnp.bfloat16)).astype(jnp.float32)
                out = jnp.einsum('qjk,kd->qjd', rounded, v_float) / total
                return out
            starts = jnp.arange(tok // qblk, dtype=jnp.int32) * qblk
            return lax.map(per_block, (q_head, starts))
        res = lax.map(per_head, (q_req, keys, vals))
        results.append(res.reshape(KVH, tok, grp, HD).transpose(1, 0, 2, 3).reshape(tok, QH * HD))
    return jnp.concatenate(results, 0)
```

```python
import functools
import math

import jax
import jax.numpy as jnp
from jax import lax
from jax.experimental import pallas as pl
from jax.experimental.pallas import tpu as pltpu
from jax.sharding import PartitionSpec as P

HD = 128
REQS = 2
BLOCK = 256
LOG2E = math.log2(math.e)
SCALE = LOG2E / math.sqrt(HD)
MESH = pl.DeviceIdType.MESH
RIGHT, LEFT, CROSS = 0, 1, 2
A, B = 0, 1
OWN, OTH = 0, 1
ONES = 16

ORDER = (
    (0, A), (0, B), (7, A), (1, A), (7, B), (1, B), (6, A), (2, A),
    (5, A), (3, A), (4, A), (5, B), (4, B), (3, B), (6, B), (2, B),
)


def dot(a, b, dims):
    return lax.dot_general(a, b, (dims, ((), ())), preferred_element_type=jnp.float32)


def table(values, index):
    out = values[0]
    for k, v in enumerate(values):
        if k:
            out = jnp.where(index == k, v, out)
    return out


def kernel(
    ring, q_in, nk, nv, k_in, v_in, owner, hist, out,
    qbuf, kg, vt, vtn, s0, s1, po, ps, ro, rs, xo, xs,
    q_send, q_recv, p_send, r_recv, x_recv,
):
    here = q_in.shape[0]
    heads = q_in.shape[1] // HD // 2
    rows = here * heads
    hist_rows = kg.shape[1]
    per_req = hist_rows // BLOCK
    blocks = per_req * REQS
    me = lax.axis_index("ctx")
    z, x = lax.div(me, 2), lax.rem(me, 2)
    right = lax.rem(z + 1, ring) * 2 + x
    left = lax.rem(z + ring - 1, ring) * 2 + x
    cross = z * 2 + 1 - x
    target = ({"ctx": right}, {"ctx": left}, {"ctx": cross})

    barrier = pltpu.get_barrier_semaphore()
    for way in (RIGHT, LEFT, CROSS):
        pl.semaphore_signal(barrier, inc=1, device_id=target[way], device_id_type=MESH)

    for g in (A, B):
        for h in range(heads):
            qbuf[0, g, OWN, pl.ds(h * here, here), :] = q_in[:, pl.ds((g * heads + h) * HD, HD)]
    pl.semaphore_wait(barrier, 3)

    def step_to(p, way):
        return (p + (ring - 1, 1, 0)[way]) % ring

    def q_copies(p, g, c, way):
        d = step_to(p, way)
        e = OTH if way == CROSS else c
        return [
            pltpu.make_async_remote_copy(
                src_ref=qbuf.at[p, g, c],
                dst_ref=qbuf.at[d, g, e],
                send_sem=q_send.at[p, g, c, way],
                recv_sem=q_recv.at[d, g, e],
                device_id=target[way],
                device_id_type=MESH,
            )
        ]

    def q_wait(p, g, c):
        pltpu.make_async_remote_copy(
            src_ref=qbuf.at[p, g, c],
            dst_ref=qbuf.at[p, g, c],
            send_sem=q_send.at[p, g, c, RIGHT],
            recv_sem=q_recv.at[p, g, c],
            device_id=target[RIGHT],
            device_id_type=MESH,
        ).wait_recv()

    def slot(p, way):
        return p if way == RIGHT else (p + 3) % ring

    def z_copies(p, g, c, way):
        d = slot(step_to(p, way), way)
        return [
            pltpu.make_async_remote_copy(
                src_ref=src.at[p, g, c],
                dst_ref=dst.at[way, d, g, c],
                send_sem=p_send.at[p, g, c, k],
                recv_sem=r_recv.at[way, d, g, c, k],
                device_id=target[way],
                device_id_type=MESH,
            )
            for k, (src, dst) in enumerate(((po, ro), (ps, rs)))
        ]

    def z_wait(p, g, c, way):
        d = slot(p, way)
        for k, dst in enumerate((ro, rs)):
            pltpu.make_async_remote_copy(
                src_ref=dst.at[way, d, g, c],
                dst_ref=dst.at[way, d, g, c],
                send_sem=p_send.at[p, g, c, k],
                recv_sem=r_recv.at[way, d, g, c, k],
                device_id=target[way],
                device_id_type=MESH,
            ).wait_recv()

    def x_copies(p, g):
        d = p if g == B else ring
        return [
            pltpu.make_async_remote_copy(
                src_ref=src.at[p, g, OTH],
                dst_ref=dst.at[d],
                send_sem=p_send.at[p, g, OTH, k],
                recv_sem=x_recv.at[d, k],
                device_id=target[CROSS],
                device_id_type=MESH,
            )
            for k, (src, dst) in enumerate(((po, xo), (ps, xs)))
        ]

    def x_wait(p, g):
        d = p if g == B else ring
        for k, dst in enumerate((xo, xs)):
            pltpu.make_async_remote_copy(
                src_ref=dst.at[d],
                dst_ref=dst.at[d],
                send_sem=p_send.at[p, g, OTH, k],
                recv_sem=x_recv.at[d, k],
                device_id=target[CROSS],
                device_id_type=MESH,
            ).wait_recv()

    started = []

    def start(make, *args):
        for copy in make(*args):
            copy.start()
        started.append((make, args))

    def merged(parts):
        tops = [s[...] for _, s in parts]
        peak = functools.reduce(jnp.maximum, tops)
        weights = [jnp.exp2(t - peak) for t in tops]
        total = sum(weights[1:], weights[0])
        share = 1.0 / total
        acc = None
        for (o, _), w in zip(parts, weights):
            term = o[...].astype(jnp.float32) * (w * share)
            acc = term if acc is None else acc + term
        return acc, peak + jnp.log(total) * LOG2E

    def fold(p, g, c, others):
        acc, lse = merged([(po.at[p, g, c], ps.at[p, g, c])] + others)
        po[p, g, c] = acc.astype(po.dtype)
        ps[p, g, c] = lse

    def from_z(p, g, c, way):
        d = slot(p, way)
        return (ro.at[way, d, g, c], rs.at[way, d, g, c])

    def need(p, g, c):
        return [(p, g, c)]

    def q_go(p, g, c, *ways):
        return need(p, g, c) + [
            lambda way=way: start(q_copies, p, g, c, way) for way in ways
        ]

    def z_go(p, g, c, way, take=True):
        def run():
            if take:
                z_wait(p, g, c, way)
                fold(p, g, c, [from_z(p, g, c, way)])
            start(z_copies, p, g, c, way)

        return [run]

    def x_go(p):
        return [lambda: start(x_copies, p, B)]

    def x_take(p):
        def run():
            x_wait(p, B)
            fold(p, B, OWN, [(xo.at[p], xs.at[p])])

        return [run]

    def unit_ready(i):
        if i >= len(ORDER):
            return []
        p, g = ORDER[i]
        return need(p, g, OWN) + need(p, g, OTH)

    events = {i: [] for i in range(-1, len(ORDER))}
    events[-1] += q_go(0, A, OWN, RIGHT, LEFT, CROSS) + q_go(0, B, OWN, RIGHT, LEFT, CROSS)
    events[-1] += q_go(0, A, OTH, RIGHT, LEFT)
    events[0] += q_go(7, A, OWN, RIGHT) + q_go(1, A, OWN, LEFT)
    events[0] += q_go(7, B, OWN, RIGHT, CROSS) + q_go(1, B, OWN, LEFT, CROSS)
    events[1] += x_go(0) + q_go(7, A, OTH, RIGHT) + q_go(1, A, OTH, LEFT)
    events[2] += q_go(6, A, OWN, RIGHT) + q_go(2, A, OWN, LEFT)
    events[3] += q_go(6, B, OWN, RIGHT, CROSS) + q_go(2, B, OWN, LEFT, CROSS)
    events[3] += q_go(6, A, OTH, RIGHT) + q_go(2, A, OTH, LEFT)
    events[4] += x_go(7) + q_go(5, A, OWN, RIGHT)
    events[5] += x_go(1) + q_go(5, B, OWN, RIGHT, CROSS) + q_go(3, B, OWN, CROSS)
    events[6] += q_go(3, A, OTH, LEFT)
    events[8] += q_go(4, B, OWN, CROSS) + x_take(7)
    events[9] += x_take(1)
    events[10] += z_go(4, A, OWN, RIGHT, False) + z_go(4, A, OTH, LEFT, False)
    events[10] += z_go(3, A, OTH, RIGHT, False) + z_go(5, A, OWN, LEFT, False)
    events[11] += x_go(5)
    events[12] += x_go(4) + z_go(3, A, OWN, RIGHT) + z_go(5, A, OTH, LEFT)
    events[13] += x_go(3) + x_take(5) + z_go(5, B, OWN, LEFT, False)
    events[13] += z_go(2, A, OTH, RIGHT) + z_go(6, A, OWN, LEFT)
    events[14] += x_go(6) + x_take(4) + z_go(4, B, OWN, RIGHT, False)
    events[14] += z_go(2, A, OWN, RIGHT) + z_go(6, A, OTH, LEFT)
    events[15] += x_go(2) + z_go(1, A, OTH, RIGHT) + z_go(7, A, OWN, LEFT)
    events[15] += x_take(3) + x_take(6) + z_go(6, B, OWN, LEFT)
    events[15] += z_go(1, A, OWN, RIGHT) + z_go(7, A, OTH, LEFT)
    events[15] += z_go(3, B, OWN, RIGHT)

    def last_a():
        z_wait(0, A, OTH, RIGHT)
        z_wait(0, A, OTH, LEFT)
        fold(0, A, OTH, [from_z(0, A, OTH, RIGHT), from_z(0, A, OTH, LEFT)])
        start(x_copies, 0, A)

    def finish(g, cross_slot):
        for way in (RIGHT, LEFT):
            z_wait(0, g, OWN, way)
        x_wait(0, g)
        acc, _ = merged(
            [
                (po.at[0, g, OWN], ps.at[0, g, OWN]),
                from_z(0, g, OWN, RIGHT),
                from_z(0, g, OWN, LEFT),
                (xo.at[cross_slot], xs.at[cross_slot]),
            ]
        )
        for h in range(heads):
            block = acc[:, h * here : (h + 1) * here]
            out[:, pl.ds((g * heads + h) * HD, HD)] = block.T

    events[15] += [last_a] + z_go(7, B, OWN, LEFT) + x_take(2) + z_go(2, B, OWN, RIGHT)
    events[15] += z_go(1, B, OWN, RIGHT)
    events[15] += [lambda: finish(A, ring), lambda: finish(B, 0)]
    events[-1] += unit_ready(0) + unit_ready(1)
    for i in range(len(ORDER)):
        events[i] += unit_ready(i + 2)
    arrived = {(0, A, OWN), (0, B, OWN)}
    for i in sorted(events):
        resolved = []
        for action in events[i]:
            if not isinstance(action, tuple):
                resolved.append(action)
            elif action not in arrived:
                arrived.add(action)
                resolved.append(functools.partial(q_wait, *action))
        events[i] = resolved

    for action in events[-1][:6]:
        action()
    lane = lax.broadcasted_iota(jnp.int32, (ONES, BLOCK), 1)
    sub = lax.broadcasted_iota(jnp.int32, (BLOCK, HD), 0)
    for r in range(REQS):
        first = None
        for b in range(per_req):
            at, base = 0, 0
            for i in range(blocks):
                here_it_is = lax.div(owner[i], 2 * ring) == r * per_req + b
                at = jnp.where(here_it_is, i, at)
                base = jnp.where(here_it_is, owner[i], base)
            base = lax.rem(base, per_req * 2 * ring) * BLOCK
            keys = k_in[at]
            vals = v_in[at]
            if first is None:
                first = keys
            left_over = hist[r] - base
            seen = sub < left_over
            kg[r, pl.ds(b * BLOCK, BLOCK), :] = jnp.where(seen, keys, first)
            vals = jnp.where(seen, vals, jnp.zeros_like(vals))
            vt[r, pl.ds(0, HD), pl.ds(b * BLOCK, BLOCK)] = vals.T
            vt[r, pl.ds(HD, ONES), pl.ds(b * BLOCK, BLOCK)] = jnp.where(
                lane < left_over, 1.0, 0.0
            ).astype(vt.dtype)
        if r == 0:
            for action in events[-1][6:9]:
                action()
    vtn[pl.ds(0, HD), :] = nv[...].T
    vtn[pl.ds(HD, ONES), :] = jnp.ones((ONES, here), vtn.dtype)
    for action in events[-1][9:]:
        action()

    step_p = [p for p, _ in ORDER]
    step_g = [g for _, g in ORDER]
    key_row = lax.broadcasted_iota(jnp.int32, (here, 2 * rows), 0)
    col = lax.broadcasted_iota(jnp.int32, (1, 2 * rows), 1)

    def place(i):
        if isinstance(i, int):
            return step_p[i], step_g[i]
        return table(step_p, i), table(step_g, i)

    def request_of(p):
        return lax.div(lax.rem(z + p, ring) * REQS, ring)

    def score(i, s):
        p, g = place(i)
        home = lax.rem(z + p, ring)
        r = request_of(p)
        q = qbuf[p, g].reshape(2 * rows, HD)
        s[pl.ds(0, hist_rows), :] = dot(kg[r], q, ((1,), (1,)))
        fresh = dot(nk[...], q, ((1,), (1,)))
        same = r == lax.div(z * REQS, ring)
        own_tok = jnp.where(same, (home * 2 + x) * here, -here)
        oth_tok = jnp.where(same, (home * 2 + 1 - x) * here, -here)
        query = jnp.where(col < rows, own_tok, oth_tok) + lax.rem(col, here)
        s[pl.ds(hist_rows, here), :] = jnp.where(me * here + key_row <= query, fresh, -1e30)

    def absorb(i, s):
        p, g = place(i)
        r = request_of(p)
        top = jnp.max(s[...], axis=0, keepdims=True) * SCALE
        probs = jnp.exp2(s[pl.ds(0, hist_rows), :] * SCALE - top).astype(jnp.bfloat16)
        fresh = jnp.exp2(s[pl.ds(hist_rows, here), :] * SCALE - top).astype(jnp.bfloat16)
        acc = dot(vt[r], probs, ((1,), (0,))) + dot(vtn[...], fresh, ((1,), (0,)))
        total = acc[HD : HD + 1]
        part = (acc[:HD] * (1.0 / total)).astype(po.dtype)
        lse = top + jnp.log(total) * LOG2E
        for c in (OWN, OTH):
            po[p, g, c] = part[:, c * rows : (c + 1) * rows]
            ps[p, g, c] = lse[:, c * rows : (c + 1) * rows]

    def after(h, half):
        for k in range(len(ORDER) // 2 - 1):
            if events[2 * k + half]:

                @pl.when(h == k)
                def _():
                    for action in events[2 * k + half]:
                        action()

    score(0, s0)

    @pl.loop(0, len(ORDER) // 2 - 1)
    def _(h):
        score(2 * h + 1, s1)
        absorb(2 * h, s0)
        after(h, 0)
        score(2 * h + 2, s0)
        absorb(2 * h + 1, s1)
        after(h, 1)

    last = len(ORDER) - 1
    score(last, s1)
    absorb(last - 1, s0)
    for action in events[last - 1]:
        action()
    absorb(last, s1)
    for action in events[last]:
        action()
    for make, args in started:
        for copy in make(*args):
            copy.wait_send()


def local(queries, new_keys, new_values, cache_keys, cache_values, block_owner, history_len):
    here, width = queries.shape
    ring = lax.axis_size("ctx") // 2
    rows = here * (width // HD) // 2
    hist_rows = cache_keys.shape[0] // REQS
    bf, f32 = jnp.bfloat16, jnp.float32
    vmem = pl.BlockSpec(memory_space=pltpu.VMEM)
    smem = pl.BlockSpec(memory_space=pltpu.SMEM)
    dma = pltpu.SemaphoreType.DMA
    all_rows = 4 * rows * ring
    keys = hist_rows + here
    return pl.pallas_call(
        functools.partial(kernel, ring),
        out_shape=jax.ShapeDtypeStruct((here, width), f32),
        in_specs=[vmem] * 5 + [smem] * 2,
        out_specs=vmem,
        scratch_shapes=[
            pltpu.VMEM((ring, 2, 2, rows, HD), bf),
            pltpu.VMEM((REQS, hist_rows, HD), bf),
            pltpu.VMEM((REQS, HD + ONES, hist_rows), bf),
            pltpu.VMEM((HD + ONES, here), bf),
            pltpu.VMEM((keys, 2 * rows), f32),
            pltpu.VMEM((keys, 2 * rows), f32),
            pltpu.VMEM((ring, 2, 2, HD, rows), bf),
            pltpu.VMEM((ring, 2, 2, 1, rows), f32),
            pltpu.VMEM((2, 4, 2, 2, HD, rows), bf),
            pltpu.VMEM((2, 4, 2, 2, 1, rows), f32),
            pltpu.VMEM((ring + 1, HD, rows), bf),
            pltpu.VMEM((ring + 1, 1, rows), f32),
            dma((ring, 2, 2, 3)),
            dma((ring, 2, 2)),
            dma((ring, 2, 2, 2)),
            dma((2, 4, 2, 2, 2)),
            dma((ring + 1, 2)),
        ],
        compiler_params=pltpu.CompilerParams(
            collective_id=0, has_side_effects=True, vmem_limit_bytes=48 * 2**20
        ),
        cost_estimate=pl.CostEstimate(
            flops=4 * all_rows * keys * HD,
            bytes_accessed=8 * hist_rows * HD + 6 * here * width,
            transcendentals=all_rows * keys,
        ),
    )(
        queries,
        new_keys,
        new_values,
        cache_keys.reshape(-1, BLOCK, HD),
        cache_values.reshape(-1, BLOCK, HD),
        block_owner,
        history_len,
    )


def solution(mesh):
    rows = P(("rep", "ctx"), "tp")
    return jax.shard_map(
        local,
        mesh=mesh,
        in_specs=(rows,) * 5 + (P(("rep", "ctx")), P("rep")),
        out_specs=rows,
        check_vma=False,
    )
```

```python
import functools
import math

import jax
import jax.numpy as jnp
from jax import lax
from jax.experimental import pallas as pl
from jax.experimental.pallas import tpu as pltpu
from jax.sharding import PartitionSpec as P

HD = 128
REQS = 2
BLOCK = 256
LOG2E = math.log2(math.e)
SCALE = LOG2E / math.sqrt(HD)
MESH = pl.DeviceIdType.MESH
A, B = 0, 1
OWN, OTH = 0, 1
ONES = 16
Q, S, F = 0, 1, 2

ORDER = (
    (1, 0),
    (7, 0),
    (0, 1),
    (2, 0),
    (7, 1),
    (6, 0),
    (3, 0),
    (5, 0),
    (1, 1),
    (5, 1),
    (4, 0),
    (4, 1),
    (3, 1),
    (6, 1),
    (2, 1),
    (0, 0),
)
BEFORE = (
    ((Q, 0, 0, 0, 1, 1), (Q, 0, 1, 0, 1, 0), (Q, 0, 0, 0, -1, 0), (Q, 0, 0, 0, 1, 0), (Q, 0, 0, 0, -1, 1), (Q, 0, 0, 0, 0, 1), (Q, 0, 1, 0, -1, 0), (Q, 0, 1, 0, 0, 1),),
    (),
    (),
    (),
    (),
    (),
    (),
    (),
    (),
    ((Q, 1, 0, 0, -1, 0), (Q, 7, 0, 1, 1, 0), (Q, 7, 1, 0, 0, 1), (Q, 7, 1, 0, 1, 0), (Q, 1, 0, 1, -1, 0),),
    ((Q, 7, 0, 0, 1, 0),),
)
AFTER = (
    ((Q, 1, 1, 0, -1, 0), (Q, 2, 0, 0, -1, 0), (Q, 1, 1, 0, 0, 1),),
    ((Q, 6, 1, 0, 1, 0), (Q, 6, 0, 1, 1, 0), (Q, 6, 1, 0, 0, 1), (Q, 2, 0, 1, -1, 0),),
    ((Q, 6, 0, 0, 1, 0), (S, 0, 1, 1, 0, 1),),
    ((Q, 2, 1, 0, -2, 0), (Q, 2, 1, 0, 0, 1), (Q, 2, 1, 0, -1, 0),),
    ((Q, 5, 1, 0, 0, 1), (S, 7, 1, 1, 0, 1),),
    ((Q, 5, 0, 1, 1, 0), (Q, 5, 0, 0, 1, 0),),
    ((S, 3, 0, 1, 1, 0), (S, 3, 0, 0, 1, 0), (Q, 4, 1, 0, 0, 1),),
    ((Q, 3, 1, 0, 0, 1), (S, 5, 0, 1, -1, 0), (S, 5, 0, 0, -1, 0),),
    ((S, 1, 1, 1, 0, 1), (F, 7, 1, 0, ((7, 1, 1, 0, 1),)), (S, 7, 1, 0, -1, 0),),
    ((F, 2, 0, 1, ((3, 0, 1, 1, 0),)), (S, 2, 0, 1, 1, 0), (S, 5, 1, 1, 0, 1),),
    ((S, 4, 0, 1, -2, 0), (S, 4, 0, 0, 2, 0),),
    ((S, 4, 1, 1, 0, 1), (F, 1, 1, 0, ((1, 1, 1, 0, 1),)), (S, 1, 1, 0, 1, 0), (F, 6, 0, 0, ((5, 0, 0, -1, 0),)), (S, 6, 0, 0, -1, 0),),
    ((S, 3, 1, 1, 0, 1), (F, 5, 1, 0, ((5, 1, 1, 0, 1),)), (S, 5, 1, 0, -1, 0), (F, 1, 0, 1, ((2, 0, 1, 1, 0),)), (S, 1, 0, 1, 1, 1),),
    ((F, 6, 0, 1, ((4, 0, 1, -2, 0), (5, 0, 1, -1, 0))), (S, 6, 0, 1, -1, 0), (F, 2, 0, 0, ((4, 0, 0, 2, 0), (3, 0, 0, 1, 0))), (S, 2, 0, 0, 1, 0), (S, 6, 1, 1, 0, 1), (F, 4, 1, 0, ((4, 1, 1, 0, 1),)), (S, 4, 1, 0, -2, 0),),
    ((S, 2, 1, 1, 0, 1), (F, 7, 0, 0, ((6, 0, 0, -1, 0),)), (S, 7, 0, 0, -1, 0), (F, 3, 1, 0, ((3, 1, 1, 0, 1),)), (S, 3, 1, 0, 1, 0),),
    ((S, 0, 0, 1, 0, 1),),
    ((F, 7, 0, 1, ((6, 0, 1, -1, 0),)), (S, 7, 0, 1, -1, 1), (F, 6, 1, 0, ((6, 1, 1, 0, 1),)), (F, 1, 0, 0, ((2, 0, 0, 1, 0),)), (S, 1, 0, 0, 1, 0), (F, 6, 1, 0, ((4, 1, 0, -2, 0), (5, 1, 0, -1, 0))), (S, 6, 1, 0, -2, 0), (F, 2, 1, 0, ((2, 1, 1, 0, 1),)), (F, 2, 1, 0, ((3, 1, 0, 1, 0),)), (S, 2, 1, 0, 2, 0),),
)
LAST = (
    ((1, 0, 0, 1, 0), (7, 0, 0, -1, 0), (1, 0, 1, 1, 1), (7, 0, 1, -1, 1), (0, 0, 1, 0, 1),),
    ((2, 1, 0, 2, 0), (1, 1, 0, 1, 0), (6, 1, 0, -2, 0), (7, 1, 0, -1, 0), (0, 1, 1, 0, 1),),
)

MESSAGES = tuple(e[1:] for es in BEFORE + AFTER for e in es if e[0] == S)
QUERIES = tuple(e[1:] for es in BEFORE + AFTER for e in es if e[0] == Q)
PARTNERS = tuple(sorted({m[3:] for m in MESSAGES + QUERIES}))


def dot(a, b, dims):
    return lax.dot_general(a, b, (dims, ((), ())), preferred_element_type=jnp.float32)


def table(values, index):
    out = values[0]
    for k, v in enumerate(values):
        if k:
            out = jnp.where(index == k, v, out)
    return out


def kernel(
    ring, q_in, nk_in, nv_in, k_hbm, v_hbm, owner, hist, out,
    qbuf, nk, nv, k_in, v_in, kg, vt, vtn, s0, s1, po, ps, ro, rs,
    l_sem, q_send, q_recv, p_send, p_recv,
):
    here, width = q_in.shape
    heads = width // HD // 2
    rows = here * heads
    hist_rows = kg.shape[1]
    per_req = hist_rows // BLOCK
    blocks = per_req * REQS
    me = lax.axis_index("ctx")
    z, x = lax.div(me, 2), lax.rem(me, 2)

    def device(steps, cross):
        column = 1 - x if cross else x
        return {"ctx": lax.rem(z + (ring + steps) % ring, ring) * 2 + column}

    loads = [
        (q_in.at[:, pl.ds((g * heads + h) * HD, HD)], qbuf.at[0, g, OWN, pl.ds(h * here, here)])
        for g in (A, B)
        for h in range(heads)
    ]
    own_queries = len(loads)
    loads += [(k_hbm, k_in), (v_hbm, v_in), (nk_in, nk), (nv_in, nv)]
    loads = [pltpu.make_async_copy(a, b, l_sem.at[i]) for i, (a, b) in enumerate(loads)]
    for load in loads:
        load.start()
    barrier = pltpu.get_barrier_semaphore()
    for partner in PARTNERS:
        pl.semaphore_signal(barrier, inc=1, device_id=device(*partner), device_id_type=MESH)
    for load in loads[:own_queries]:
        load.wait()
    pl.semaphore_wait(barrier, len(PARTNERS))

    def q_copy(n):
        p, g, c, steps, cross = QUERIES[n]
        d = (p - steps) % ring
        e = OTH if cross else c
        return pltpu.make_async_remote_copy(
            src_ref=qbuf.at[p, g, c],
            dst_ref=qbuf.at[d, g, e],
            send_sem=q_send.at[n],
            recv_sem=q_recv.at[d, g, e],
            device_id=device(steps, cross),
            device_id_type=MESH,
        )

    def q_wait(p, g, c):
        pltpu.make_async_remote_copy(
            src_ref=qbuf.at[p, g, c],
            dst_ref=qbuf.at[p, g, c],
            send_sem=q_send.at[0],
            recv_sem=q_recv.at[p, g, c],
            device_id=device(*PARTNERS[0]),
            device_id_type=MESH,
        ).wait_recv()

    def p_copies(n):
        p, g, c, steps, cross = MESSAGES[n]
        return [
            pltpu.make_async_remote_copy(
                src_ref=src.at[p, g, c],
                dst_ref=dst.at[n],
                send_sem=p_send.at[n, k],
                recv_sem=p_recv.at[n, k],
                device_id=device(steps, cross),
                device_id_type=MESH,
            )
            for k, (src, dst) in enumerate(((po, ro), (ps, rs)))
        ]

    def merged(parts):
        tops = [s[...] for _, s in parts]
        peak = functools.reduce(jnp.maximum, tops)
        weights = [jnp.exp2(t - peak) for t in tops]
        total = sum(weights[1:], weights[0])
        share = 1.0 / total
        acc = None
        for (o, _), w in zip(parts, weights):
            term = o[...].astype(jnp.float32) * (w * share)
            acc = term if acc is None else acc + term
        return acc, peak + jnp.log(total) * LOG2E

    def take(p, g, c, messages):
        parts = [(po.at[p, g, c], ps.at[p, g, c])]
        for message in messages:
            n = MESSAGES.index(message)
            for copy in p_copies(n):
                copy.wait_recv()
            parts.append((ro.at[n], rs.at[n]))
        return merged(parts)

    def finish(g):
        acc, _ = take(0, g, OWN, LAST[g])
        for h in range(heads):
            out[:, pl.ds((g * heads + h) * HD, HD)] = acc[:, h * here : (h + 1) * here].T

    def act(event):
        kind, *rest = event
        if kind == Q:
            q_copy(QUERIES.index(tuple(rest))).start()
        elif kind == S:
            for copy in p_copies(MESSAGES.index(tuple(rest))):
                copy.start()
        elif kind == F:
            p, g, c, messages = rest
            acc, lse = take(p, g, c, messages)
            po[p, g, c] = acc.astype(po.dtype)
            ps[p, g, c] = lse
        else:
            q_wait(*rest)

    arrived = {(0, A, OWN), (0, B, OWN)}

    def with_waits(events, unit):
        result = []
        needs = [(e, [e[1:4]] if e[0] == Q else []) for e in events]
        if unit < len(ORDER):
            needs.append((None, [ORDER[unit] + (c,) for c in (OWN, OTH)]))
        for event, blocks_of in needs:
            for block in blocks_of:
                if block not in arrived:
                    arrived.add(block)
                    result.append((None,) + block)
            if event is not None:
                result.append(event)
        return result

    none = len(ORDER)
    before = [with_waits(es, none) for es in BEFORE[:-2]]
    before += [with_waits(BEFORE[-2], 0), with_waits(BEFORE[-1], 1)]
    after = [with_waits(es, i + 2) for i, es in enumerate(AFTER)]

    for event in before[0]:
        act(event)
    for load in loads[own_queries:]:
        load.wait()

    lane = lax.broadcasted_iota(jnp.int32, (ONES, BLOCK), 1)
    sub = lax.broadcasted_iota(jnp.int32, (BLOCK, HD), 0)
    parts = len(before) - 3
    for i in range(blocks):
        r, b = i // per_req, i % per_req
        at, base = 0, 0
        for j in range(blocks):
            found = lax.div(owner[j], 2 * ring) == i
            at = jnp.where(found, j, at)
            base = jnp.where(found, owner[j], base)
        base = lax.rem(base, per_req * 2 * ring) * BLOCK
        keys = k_in[at]
        vals = v_in[at]
        if b == 0:
            first = keys
        left_over = hist[r] - base
        seen = sub < left_over
        kg[r, pl.ds(b * BLOCK, BLOCK), :] = jnp.where(seen, keys, first)
        vals = jnp.where(seen, vals, jnp.zeros_like(vals))
        vt[r, pl.ds(0, HD), pl.ds(b * BLOCK, BLOCK)] = vals.T
        vt[r, pl.ds(HD, ONES), pl.ds(b * BLOCK, BLOCK)] = jnp.where(
            lane < left_over, 1.0, 0.0
        ).astype(vt.dtype)
        if (i + 1) * parts % blocks == 0:
            for event in before[(i + 1) * parts // blocks]:
                act(event)
    vtn[pl.ds(0, HD), :] = nv[...].T
    vtn[pl.ds(HD, ONES), :] = jnp.ones((ONES, here), vtn.dtype)
    for event in before[-2]:
        act(event)

    step_p = [p for p, _ in ORDER]
    step_g = [g for _, g in ORDER]
    key_row = lax.broadcasted_iota(jnp.int32, (here, 2 * rows), 0)
    col = lax.broadcasted_iota(jnp.int32, (1, 2 * rows), 1)

    def place(i):
        if isinstance(i, int):
            return step_p[i], step_g[i]
        return table(step_p, i), table(step_g, i)

    def request_of(p):
        return lax.div(lax.rem(z + p, ring) * REQS, ring)

    def score(i, s):
        p, g = place(i)
        home = lax.rem(z + p, ring)
        r = request_of(p)
        q = qbuf[p, g].reshape(2 * rows, HD)
        s[pl.ds(0, hist_rows), :] = dot(kg[r], q, ((1,), (1,)))
        fresh = dot(nk[...], q, ((1,), (1,)))
        same = r == lax.div(z * REQS, ring)
        own_tok = jnp.where(same, (home * 2 + x) * here, -here)
        oth_tok = jnp.where(same, (home * 2 + 1 - x) * here, -here)
        query = jnp.where(col < rows, own_tok, oth_tok) + lax.rem(col, here)
        s[pl.ds(hist_rows, here), :] = jnp.where(me * here + key_row <= query, fresh, -1e30)

    def absorb(i, s):
        p, g = place(i)
        r = request_of(p)
        top = jnp.max(s[...], axis=0, keepdims=True) * SCALE
        probs = jnp.exp2(s[pl.ds(0, hist_rows), :] * SCALE - top).astype(jnp.bfloat16)
        fresh = jnp.exp2(s[pl.ds(hist_rows, here), :] * SCALE - top).astype(jnp.bfloat16)
        acc = dot(vt[r], probs, ((1,), (0,))) + dot(vtn[...], fresh, ((1,), (0,)))
        total = acc[HD : HD + 1]
        part = (acc[:HD] * (1.0 / total)).astype(po.dtype)
        lse = top + jnp.log(total) * LOG2E
        for c in (OWN, OTH):
            po[p, g, c] = part[:, c * rows : (c + 1) * rows]
            ps[p, g, c] = lse[:, c * rows : (c + 1) * rows]

    def react(h, half):
        for k in range(len(ORDER) // 2 - 1):
            if after[2 * k + half]:

                @pl.when(h == k)
                def _():
                    for event in after[2 * k + half]:
                        act(event)

    score(0, s0)
    for event in before[-1]:
        act(event)

    @pl.loop(0, len(ORDER) // 2 - 1)
    def _(h):
        score(2 * h + 1, s1)
        absorb(2 * h, s0)
        react(h, 0)
        score(2 * h + 2, s0)
        absorb(2 * h + 1, s1)
        react(h, 1)

    last = len(ORDER) - 1
    score(last, s1)
    absorb(last - 1, s0)
    for event in after[last - 1]:
        act(event)
    absorb(last, s1)
    for event in after[last] + after[last + 1]:
        act(event)
    finish(A)
    finish(B)
    for n in range(len(QUERIES)):
        q_copy(n).wait_send()
    for n in range(len(MESSAGES)):
        for copy in p_copies(n):
            copy.wait_send()


def local(queries, new_keys, new_values, cache_keys, cache_values, block_owner, history_len):
    here, width = queries.shape
    ring = lax.axis_size("ctx") // 2
    heads = width // HD
    rows = here * heads // 2
    slots = cache_keys.shape[0]
    hist_rows = slots // REQS
    bf, f32 = jnp.bfloat16, jnp.float32
    hbm = pl.BlockSpec(memory_space=pl.ANY)
    smem = pl.BlockSpec(memory_space=pltpu.SMEM)
    dma = pltpu.SemaphoreType.DMA
    all_rows = 4 * rows * ring
    keys = hist_rows + here
    return pl.pallas_call(
        functools.partial(kernel, ring),
        out_shape=jax.ShapeDtypeStruct((here, width), f32),
        in_specs=[hbm] * 5 + [smem] * 2,
        out_specs=pl.BlockSpec(memory_space=pltpu.VMEM),
        scratch_shapes=[
            pltpu.VMEM((ring, 2, 2, rows, HD), bf),
            pltpu.VMEM((here, HD), bf),
            pltpu.VMEM((here, HD), bf),
            pltpu.VMEM((slots // BLOCK, BLOCK, HD), bf),
            pltpu.VMEM((slots // BLOCK, BLOCK, HD), bf),
            pltpu.VMEM((REQS, hist_rows, HD), bf),
            pltpu.VMEM((REQS, HD + ONES, hist_rows), bf),
            pltpu.VMEM((HD + ONES, here), bf),
            pltpu.VMEM((keys, 2 * rows), f32),
            pltpu.VMEM((keys, 2 * rows), f32),
            pltpu.VMEM((ring, 2, 2, HD, rows), bf),
            pltpu.VMEM((ring, 2, 2, 1, rows), f32),
            pltpu.VMEM((len(MESSAGES), HD, rows), bf),
            pltpu.VMEM((len(MESSAGES), 1, rows), f32),
            dma((heads + 4,)),
            dma((len(QUERIES),)),
            dma((ring, 2, 2)),
            dma((len(MESSAGES), 2)),
            dma((len(MESSAGES), 2)),
        ],
        compiler_params=pltpu.CompilerParams(
            collective_id=0, has_side_effects=True, vmem_limit_bytes=52 * 2**20
        ),
        cost_estimate=pl.CostEstimate(
            flops=4 * all_rows * keys * HD,
            bytes_accessed=4 * slots * HD + 6 * here * width,
            transcendentals=all_rows * keys,
        ),
    )(
        queries,
        new_keys,
        new_values,
        cache_keys.reshape(-1, BLOCK, HD),
        cache_values.reshape(-1, BLOCK, HD),
        block_owner,
        history_len,
    )


def solution(mesh):
    rows = P(("rep", "ctx"), "tp")
    return jax.shard_map(
        local,
        mesh=mesh,
        in_specs=(rows,) * 5 + (P(("rep", "ctx")), P("rep")),
        out_specs=rows,
        check_vma=False,
    )
```

```python
import functools
import math

import jax
import jax.numpy as jnp
from jax import lax
from jax.experimental import pallas as pl
from jax.experimental.pallas import tpu as pltpu
from jax.sharding import PartitionSpec as P

HD = 128
REQS = 2
BLOCK = 256
LOG2E = math.log2(math.e)
SCALE = LOG2E / math.sqrt(HD)
MESH = pl.DeviceIdType.MESH
A, B = 0, 1
OWN, OTH = 0, 1
ONES = 16
Q, S, F = 0, 1, 2

ORDER = (
    (1, 0),
    (7, 0),
    (0, 1),
    (2, 0),
    (7, 1),
    (6, 0),
    (3, 0),
    (5, 0),
    (1, 1),
    (5, 1),
    (4, 0),
    (4, 1),
    (3, 1),
    (6, 1),
    (2, 1),
    (0, 0),
)
BEFORE = (
    ((Q, 0, 0, 0, 1, 1), (Q, 0, 1, 0, 1, 0), (Q, 0, 0, 0, -1, 0), (Q, 0, 0, 0, 1, 0), (Q, 0, 0, 0, -1, 1), (Q, 0, 0, 0, 0, 1), (Q, 0, 1, 0, -1, 0), (Q, 0, 1, 0, 0, 1),),
    (),
    (),
    (),
    (),
    (),
    (),
    (),
    (),
    ((Q, 1, 0, 0, -1, 0), (Q, 7, 0, 1, 1, 0), (Q, 7, 1, 0, 0, 1), (Q, 7, 1, 0, 1, 0), (Q, 1, 0, 1, -1, 0),),
    ((Q, 7, 0, 0, 1, 0),),
)
AFTER = (
    ((Q, 1, 1, 0, -1, 0), (Q, 2, 0, 0, -1, 0), (Q, 1, 1, 0, 0, 1),),
    ((Q, 6, 1, 0, 1, 0), (Q, 6, 0, 1, 1, 0), (Q, 6, 1, 0, 0, 1), (Q, 2, 0, 1, -1, 0),),
    ((Q, 6, 0, 0, 1, 0), (S, 0, 1, 1, 0, 1),),
    ((Q, 2, 1, 0, -2, 0), (Q, 2, 1, 0, 0, 1), (Q, 2, 1, 0, -1, 0),),
    ((Q, 5, 1, 0, 0, 1), (S, 7, 1, 1, 0, 1),),
    ((Q, 5, 0, 1, 1, 0), (Q, 5, 0, 0, 1, 0),),
    ((S, 3, 0, 1, 1, 0), (S, 3, 0, 0, 1, 0), (Q, 4, 1, 0, 0, 1),),
    ((Q, 3, 1, 0, 0, 1), (S, 5, 0, 1, -1, 0), (S, 5, 0, 0, -1, 0),),
    ((S, 1, 1, 1, 0, 1), (F, 7, 1, 0, ((7, 1, 1, 0, 1),)), (S, 7, 1, 0, -1, 0),),
    ((F, 2, 0, 1, ((3, 0, 1, 1, 0),)), (S, 2, 0, 1, 1, 0), (S, 5, 1, 1, 0, 1),),
    ((S, 4, 0, 1, -2, 0), (S, 4, 0, 0, 2, 0),),
    ((S, 4, 1, 1, 0, 1), (F, 1, 1, 0, ((1, 1, 1, 0, 1),)), (S, 1, 1, 0, 1, 0), (F, 6, 0, 0, ((5, 0, 0, -1, 0),)), (S, 6, 0, 0, -1, 0),),
    ((S, 3, 1, 1, 0, 1), (F, 5, 1, 0, ((5, 1, 1, 0, 1),)), (S, 5, 1, 0, -1, 0), (F, 1, 0, 1, ((2, 0, 1, 1, 0),)), (S, 1, 0, 1, 1, 1),),
    ((F, 6, 0, 1, ((4, 0, 1, -2, 0), (5, 0, 1, -1, 0))), (S, 6, 0, 1, -1, 0), (F, 2, 0, 0, ((4, 0, 0, 2, 0), (3, 0, 0, 1, 0))), (S, 2, 0, 0, 1, 0), (S, 6, 1, 1, 0, 1), (F, 4, 1, 0, ((4, 1, 1, 0, 1),)), (S, 4, 1, 0, -2, 0),),
    ((S, 2, 1, 1, 0, 1), (F, 7, 0, 0, ((6, 0, 0, -1, 0),)), (S, 7, 0, 0, -1, 0), (F, 3, 1, 0, ((3, 1, 1, 0, 1),)), (S, 3, 1, 0, 1, 0),),
    ((S, 0, 0, 1, 0, 1),),
    ((F, 7, 0, 1, ((6, 0, 1, -1, 0),)), (S, 7, 0, 1, -1, 1), (F, 6, 1, 0, ((6, 1, 1, 0, 1),)), (F, 1, 0, 0, ((2, 0, 0, 1, 0),)), (S, 1, 0, 0, 1, 0), (F, 6, 1, 0, ((4, 1, 0, -2, 0), (5, 1, 0, -1, 0))), (S, 6, 1, 0, -2, 0), (F, 2, 1, 0, ((2, 1, 1, 0, 1),)), (F, 2, 1, 0, ((3, 1, 0, 1, 0),)), (S, 2, 1, 0, 2, 0),),
)
LAST = (
    ((1, 0, 0, 1, 0), (7, 0, 0, -1, 0), (1, 0, 1, 1, 1), (7, 0, 1, -1, 1), (0, 0, 1, 0, 1),),
    ((2, 1, 0, 2, 0), (1, 1, 0, 1, 0), (6, 1, 0, -2, 0), (7, 1, 0, -1, 0), (0, 1, 1, 0, 1),),
)

MESSAGES = tuple(e[1:] for es in BEFORE + AFTER for e in es if e[0] == S)
QUERIES = tuple(e[1:] for es in BEFORE + AFTER for e in es if e[0] == Q)
PARTNERS = tuple(sorted({m[3:] for m in MESSAGES + QUERIES}))


def dot(a, b, dims):
    return lax.dot_general(a, b, (dims, ((), ())), preferred_element_type=jnp.float32)


def table(values, index):
    out = values[0]
    for k, v in enumerate(values):
        if k:
            out = jnp.where(index == k, v, out)
    return out


def kernel(
    ring, q_in, nk_in, nv_in, k_hbm, v_hbm, owner_in, hist_in, out,
    qbuf, owner, hist, nk, nv, k_in, v_in, kg, vt, vtn, s0, s1, po, ps, ro, rs,
    l_sem, q_send, q_recv, p_send, p_recv,
):
    here, width = q_in.shape
    heads = width // HD // 2
    rows = here * heads
    hist_rows = kg.shape[1]
    per_req = hist_rows // BLOCK
    blocks = per_req * REQS
    me = lax.axis_index("ctx")
    z, x = lax.div(me, 2), lax.rem(me, 2)

    def device(steps, cross):
        column = 1 - x if cross else x
        return {"ctx": lax.rem(z + (ring + steps) % ring, ring) * 2 + column}

    loads = [
        (q_in.at[:, pl.ds((g * heads + h) * HD, HD)], qbuf.at[0, g, OWN, pl.ds(h * here, here)])
        for g in (A, B)
        for h in range(heads)
    ]
    own_queries = len(loads)
    loads += [(owner_in, owner), (hist_in, hist)]
    loads += [(k_hbm, k_in), (v_hbm, v_in), (nk_in, nk), (nv_in, nv)]
    loads = [pltpu.make_async_copy(a, b, l_sem.at[i]) for i, (a, b) in enumerate(loads)]
    for load in loads:
        load.start()
    barrier = pltpu.get_barrier_semaphore()
    for partner in PARTNERS:
        pl.semaphore_signal(barrier, inc=1, device_id=device(*partner), device_id_type=MESH)
    for load in loads[:own_queries]:
        load.wait()
    pl.semaphore_wait(barrier, len(PARTNERS))

    def q_copy(n):
        p, g, c, steps, cross = QUERIES[n]
        d = (p - steps) % ring
        e = OTH if cross else c
        return pltpu.make_async_remote_copy(
            src_ref=qbuf.at[p, g, c],
            dst_ref=qbuf.at[d, g, e],
            send_sem=q_send.at[n],
            recv_sem=q_recv.at[d, g, e],
            device_id=device(steps, cross),
            device_id_type=MESH,
        )

    def q_wait(p, g, c):
        pltpu.make_async_remote_copy(
            src_ref=qbuf.at[p, g, c],
            dst_ref=qbuf.at[p, g, c],
            send_sem=q_send.at[0],
            recv_sem=q_recv.at[p, g, c],
            device_id=device(*PARTNERS[0]),
            device_id_type=MESH,
        ).wait_recv()

    def p_copies(n):
        p, g, c, steps, cross = MESSAGES[n]
        return [
            pltpu.make_async_remote_copy(
                src_ref=src.at[p, g, c],
                dst_ref=dst.at[n],
                send_sem=p_send.at[n, k],
                recv_sem=p_recv.at[n, k],
                device_id=device(steps, cross),
                device_id_type=MESH,
            )
            for k, (src, dst) in enumerate(((po, ro), (ps, rs)))
        ]

    def merged(parts):
        tops = [s[...] for _, s in parts]
        peak = functools.reduce(jnp.maximum, tops)
        weights = [jnp.exp2(t - peak) for t in tops]
        total = sum(weights[1:], weights[0])
        share = 1.0 / total
        acc = None
        for (o, _), w in zip(parts, weights):
            term = o[...].astype(jnp.float32) * (w * share)
            acc = term if acc is None else acc + term
        return acc, peak + jnp.log(total) * LOG2E

    def take(p, g, c, messages):
        parts = [(po.at[p, g, c], ps.at[p, g, c])]
        for message in messages:
            n = MESSAGES.index(message)
            for copy in p_copies(n):
                copy.wait_recv()
            parts.append((ro.at[n], rs.at[n]))
        return merged(parts)

    def finish(g):
        acc, _ = take(0, g, OWN, LAST[g])
        for h in range(heads):
            out[:, pl.ds((g * heads + h) * HD, HD)] = acc[:, h * here : (h + 1) * here].T

    def act(event):
        kind, *rest = event
        if kind == Q:
            q_copy(QUERIES.index(tuple(rest))).start()
        elif kind == S:
            for copy in p_copies(MESSAGES.index(tuple(rest))):
                copy.start()
        elif kind == F:
            p, g, c, messages = rest
            acc, lse = take(p, g, c, messages)
            po[p, g, c] = acc.astype(po.dtype)
            ps[p, g, c] = lse
        else:
            q_wait(*rest)

    arrived = {(0, A, OWN), (0, B, OWN)}

    def with_waits(events, unit):
        result = []
        needs = [(e, [e[1:4]] if e[0] == Q else []) for e in events]
        if unit < len(ORDER):
            needs.append((None, [ORDER[unit] + (c,) for c in (OWN, OTH)]))
        for event, blocks_of in needs:
            for block in blocks_of:
                if block not in arrived:
                    arrived.add(block)
                    result.append((None,) + block)
            if event is not None:
                result.append(event)
        return result

    none = len(ORDER)
    before = [with_waits(es, none) for es in BEFORE[:-2]]
    before += [with_waits(BEFORE[-2], 0), with_waits(BEFORE[-1], 1)]
    after = [with_waits(es, i + 2) for i, es in enumerate(AFTER)]

    for event in before[0]:
        act(event)
    for load in loads[own_queries:]:
        load.wait()

    lane = lax.broadcasted_iota(jnp.int32, (ONES, BLOCK), 1)
    sub = lax.broadcasted_iota(jnp.int32, (BLOCK, HD), 0)
    parts = len(before) - 3
    for i in range(blocks):
        r, b = i // per_req, i % per_req
        at, base = 0, 0
        for j in range(blocks):
            found = lax.div(owner[j], 2 * ring) == i
            at = jnp.where(found, j, at)
            base = jnp.where(found, owner[j], base)
        base = lax.rem(base, per_req * 2 * ring) * BLOCK
        keys = k_in[at]
        vals = v_in[at]
        if b == 0:
            first = keys
        left_over = hist[r] - base
        seen = sub < left_over
        kg[r, pl.ds(b * BLOCK, BLOCK), :] = jnp.where(seen, keys, first)
        vals = jnp.where(seen, vals, jnp.zeros_like(vals))
        vt[r, pl.ds(0, HD), pl.ds(b * BLOCK, BLOCK)] = vals.T
        vt[r, pl.ds(HD, ONES), pl.ds(b * BLOCK, BLOCK)] = jnp.where(
            lane < left_over, 1.0, 0.0
        ).astype(vt.dtype)
        if (i + 1) * parts % blocks == 0:
            for event in before[(i + 1) * parts // blocks]:
                act(event)
    vtn[pl.ds(0, HD), :] = nv[...].T
    vtn[pl.ds(HD, ONES), :] = jnp.ones((ONES, here), vtn.dtype)
    for event in before[-2]:
        act(event)

    step_p = [p for p, _ in ORDER]
    step_g = [g for _, g in ORDER]
    key_row = lax.broadcasted_iota(jnp.int32, (here, 2 * rows), 0)
    col = lax.broadcasted_iota(jnp.int32, (1, 2 * rows), 1)

    def place(i):
        if isinstance(i, int):
            return step_p[i], step_g[i]
        return table(step_p, i), table(step_g, i)

    def request_of(p):
        return lax.div(lax.rem(z + p, ring) * REQS, ring)

    def score(i, s):
        p, g = place(i)
        home = lax.rem(z + p, ring)
        r = request_of(p)
        q = qbuf[p, g].reshape(2 * rows, HD)
        s[pl.ds(0, hist_rows), :] = dot(kg[r], q, ((1,), (1,)))
        fresh = dot(nk[...], q, ((1,), (1,)))
        same = r == lax.div(z * REQS, ring)
        own_tok = jnp.where(same, (home * 2 + x) * here, -here)
        oth_tok = jnp.where(same, (home * 2 + 1 - x) * here, -here)
        query = jnp.where(col < rows, own_tok, oth_tok) + lax.rem(col, here)
        s[pl.ds(hist_rows, here), :] = jnp.where(me * here + key_row <= query, fresh, -1e30)

    def absorb(i, s):
        p, g = place(i)
        r = request_of(p)
        top = jnp.max(s[...], axis=0, keepdims=True) * SCALE
        probs = jnp.exp2(s[pl.ds(0, hist_rows), :] * SCALE - top).astype(jnp.bfloat16)
        fresh = jnp.exp2(s[pl.ds(hist_rows, here), :] * SCALE - top).astype(jnp.bfloat16)
        acc = dot(vt[r], probs, ((1,), (0,))) + dot(vtn[...], fresh, ((1,), (0,)))
        total = acc[HD : HD + 1]
        part = (acc[:HD] * (1.0 / total)).astype(po.dtype)
        lse = top + jnp.log(total) * LOG2E
        for c in (OWN, OTH):
            po[p, g, c] = part[:, c * rows : (c + 1) * rows]
            ps[p, g, c] = lse[:, c * rows : (c + 1) * rows]

    def react(h, half):
        for k in range(len(ORDER) // 2 - 1):
            if after[2 * k + half]:

                @pl.when(h == k)
                def _():
                    for event in after[2 * k + half]:
                        act(event)

    score(0, s0)
    for event in before[-1]:
        act(event)

    @pl.loop(0, len(ORDER) // 2 - 1)
    def _(h):
        score(2 * h + 1, s1)
        absorb(2 * h, s0)
        react(h, 0)
        score(2 * h + 2, s0)
        absorb(2 * h + 1, s1)
        react(h, 1)

    last = len(ORDER) - 1
    score(last, s1)
    absorb(last - 1, s0)
    for event in after[last - 1]:
        act(event)
    absorb(last, s1)
    for event in after[last] + after[last + 1]:
        act(event)
    finish(A)
    finish(B)
    for n in range(len(QUERIES)):
        q_copy(n).wait_send()
    for n in range(len(MESSAGES)):
        for copy in p_copies(n):
            copy.wait_send()


def local(queries, new_keys, new_values, cache_keys, cache_values, block_owner, history_len):
    here, width = queries.shape
    ring = lax.axis_size("ctx") // 2
    heads = width // HD
    rows = here * heads // 2
    slots = cache_keys.shape[0]
    hist_rows = slots // REQS
    bf, f32 = jnp.bfloat16, jnp.float32
    hbm = pl.BlockSpec(memory_space=pltpu.HBM)
    dma = pltpu.SemaphoreType.DMA
    all_rows = 4 * rows * ring
    keys = hist_rows + here
    return pl.pallas_call(
        functools.partial(kernel, ring),
        out_shape=jax.ShapeDtypeStruct((here, width), f32),
        in_specs=[hbm] * 7,
        out_specs=pl.BlockSpec(memory_space=pltpu.VMEM),
        scratch_shapes=[
            pltpu.VMEM((ring, 2, 2, rows, HD), bf),
            pltpu.SMEM(block_owner.shape, jnp.int32),
            pltpu.SMEM(history_len.shape, jnp.int32),
            pltpu.VMEM((here, HD), bf),
            pltpu.VMEM((here, HD), bf),
            pltpu.VMEM((slots // BLOCK, BLOCK, HD), bf),
            pltpu.VMEM((slots // BLOCK, BLOCK, HD), bf),
            pltpu.VMEM((REQS, hist_rows, HD), bf),
            pltpu.VMEM((REQS, HD + ONES, hist_rows), bf),
            pltpu.VMEM((HD + ONES, here), bf),
            pltpu.VMEM((keys, 2 * rows), f32),
            pltpu.VMEM((keys, 2 * rows), f32),
            pltpu.VMEM((ring, 2, 2, HD, rows), bf),
            pltpu.VMEM((ring, 2, 2, 1, rows), f32),
            pltpu.VMEM((len(MESSAGES), HD, rows), bf),
            pltpu.VMEM((len(MESSAGES), 1, rows), f32),
            dma((heads + 6,)),
            dma((len(QUERIES),)),
            dma((ring, 2, 2)),
            dma((len(MESSAGES), 2)),
            dma((len(MESSAGES), 2)),
        ],
        compiler_params=pltpu.CompilerParams(
            collective_id=0, has_side_effects=True, vmem_limit_bytes=63 * 2**20
        ),
        cost_estimate=pl.CostEstimate(
            flops=4 * all_rows * keys * HD,
            bytes_accessed=4 * slots * HD + 6 * here * width,
            transcendentals=all_rows * keys,
        ),
    )(
        queries,
        new_keys,
        new_values,
        cache_keys.reshape(-1, BLOCK, HD),
        cache_values.reshape(-1, BLOCK, HD),
        block_owner,
        history_len,
    )


def solution(mesh):
    rows = P(("rep", "ctx"), "tp")
    return jax.shard_map(
        local,
        mesh=mesh,
        in_specs=(rows,) * 5 + (P(("rep", "ctx")), P("rep")),
        out_specs=rows,
        check_vma=False,
    )
```

```python
import functools
import math

import jax
import jax.numpy as jnp
from jax import lax
from jax.experimental import pallas as pl
from jax.experimental.pallas import tpu as pltpu
from jax.sharding import PartitionSpec as P

HD = 128
REQS = 2
BLOCK = 256
LOG2E = math.log2(math.e)
SCALE = LOG2E / math.sqrt(HD)
MESH = pl.DeviceIdType.MESH
A, B = 0, 1
OWN, OTH = 0, 1
ONES = 16
Q, S, F = 0, 1, 2

ORDER = (
    (1, 0),
    (0, 1),
    (7, 0),
    (7, 1),
    (2, 0),
    (6, 0),
    (6, 1),
    (3, 0),
    (5, 0),
    (5, 1),
    (4, 0),
    (4, 1),
    (3, 1),
    (1, 1),
    (2, 1),
    (0, 0),
)
BEFORE = (
    ((Q, 0, 1, 0, 1, 0), (Q, 0, 0, 0, -1, 1), (Q, 0, 0, 0, -1, 0), (Q, 0, 1, 0, 0, 1), (Q, 0, 1, 0, -1, 0), (Q, 0, 0, 0, 1, 0), (Q, 0, 0, 0, 1, 1), (Q, 0, 0, 0, 0, 1),),
    (),
    (),
    (),
    (),
    (),
    (),
    (),
    (),
    ((Q, 7, 1, 0, 0, 1), (Q, 7, 1, 0, 1, 0), (Q, 1, 0, 1, -1, 0), (Q, 7, 0, 0, 1, 0), (Q, 1, 0, 0, -1, 0),),
    (),
)
AFTER = (
    ((Q, 7, 0, 1, 1, 0), (Q, 1, 1, 0, 0, 1), (Q, 1, 1, 0, -1, 0),),
    ((Q, 6, 1, 0, 0, 1), (Q, 2, 0, 1, -1, 0), (Q, 6, 1, 0, 1, 0), (S, 0, 1, 1, 0, 1), (Q, 6, 0, 0, 1, 0),),
    ((Q, 2, 0, 0, -1, 0),),
    ((Q, 2, 1, 0, 0, 1), (Q, 6, 0, 1, 1, 0), (Q, 2, 1, 0, -1, 0), (S, 7, 1, 1, 0, 1),),
    ((Q, 3, 0, 1, -1, 0), (Q, 5, 1, 0, 0, 1), (Q, 5, 1, 0, 1, 0), (Q, 5, 1, 0, 1, 1),),
    ((Q, 3, 0, 0, -1, 0),),
    ((Q, 3, 1, 0, 0, 1), (S, 6, 1, 1, 0, 1),),
    ((S, 3, 0, 0, 1, 0), (S, 3, 0, 1, 1, 0), (F, 7, 1, 0, ((7, 1, 1, 0, 1),)), (S, 7, 1, 0, -1, 0),),
    ((S, 5, 0, 0, -1, 0), (S, 5, 0, 1, -1, 0),),
    ((S, 5, 1, 1, 0, 1),),
    ((S, 4, 0, 0, 2, 0), (S, 4, 0, 1, -2, 0), (F, 6, 1, 0, ((6, 1, 1, 0, 1),)),),
    ((F, 2, 0, 1, ((3, 0, 1, 1, 0),)), (S, 2, 0, 1, 1, 0), (S, 4, 1, 1, 0, 1), (F, 6, 0, 0, ((5, 0, 0, -1, 0),)), (S, 6, 0, 0, -1, 0),),
    ((F, 5, 1, 0, ((5, 1, 1, 0, 1),)), (S, 5, 1, 0, -1, 0), (S, 3, 1, 1, 0, 1),),
    ((F, 6, 0, 1, ((4, 0, 1, -2, 0), (5, 0, 1, -1, 0))), (S, 6, 0, 1, -1, 0), (F, 2, 0, 0, ((4, 0, 0, 2, 0), (3, 0, 0, 1, 0))), (S, 2, 0, 0, 1, 0), (S, 1, 1, 1, 0, 1),),
    ((F, 4, 1, 0, ((4, 1, 1, 0, 1),)), (F, 1, 0, 1, ((2, 0, 1, 1, 0),)), (S, 1, 0, 1, 1, 1), (S, 4, 1, 0, -2, 0), (S, 2, 1, 1, 0, 1), (F, 7, 0, 0, ((6, 0, 0, -1, 0),)), (S, 7, 0, 0, -1, 0),),
    ((F, 3, 1, 0, ((3, 1, 1, 0, 1),)), (S, 3, 1, 0, 1, 0), (S, 0, 0, 1, 0, 1),),
    ((F, 1, 0, 0, ((2, 0, 0, 1, 0),)), (S, 1, 0, 0, 1, 0), (F, 1, 1, 0, ((1, 1, 1, 0, 1),)), (S, 1, 1, 0, 1, 0), (F, 7, 0, 1, ((6, 0, 1, -1, 0),)), (S, 7, 0, 1, -1, 1), (F, 6, 1, 0, ((4, 1, 0, -2, 0), (5, 1, 0, -1, 0))), (S, 6, 1, 0, -2, 0), (F, 2, 1, 0, ((2, 1, 1, 0, 1),)), (F, 2, 1, 0, ((3, 1, 0, 1, 0),)), (S, 2, 1, 0, 2, 0),),
)
LAST = (
    ((1, 0, 0, 1, 0), (7, 0, 0, -1, 0), (1, 0, 1, 1, 1), (7, 0, 1, -1, 1), (0, 0, 1, 0, 1),),
    ((2, 1, 0, 2, 0), (1, 1, 0, 1, 0), (6, 1, 0, -2, 0), (7, 1, 0, -1, 0), (0, 1, 1, 0, 1),),
)

MESSAGES = tuple(e[1:] for es in BEFORE + AFTER for e in es if e[0] == S)
QUERIES = tuple(e[1:] for es in BEFORE + AFTER for e in es if e[0] == Q)
PARTNERS = tuple(sorted({m[3:] for m in MESSAGES + QUERIES}))


def dot(a, b, dims):
    return lax.dot_general(a, b, (dims, ((), ())), preferred_element_type=jnp.float32)


def table(values, index):
    out = values[0]
    for k, v in enumerate(values):
        if k:
            out = jnp.where(index == k, v, out)
    return out


def kernel(
    ring, q_in, nk_in, nv_in, k_hbm, v_hbm, owner_in, hist_in, out,
    qbuf, owner, hist, nk, nv, k_in, v_in, kg, vt, vtn, s0, s1, po, ps, ro, rs,
    l_sem, q_send, q_recv, p_send, p_recv,
):
    here, width = q_in.shape
    heads = width // HD // 2
    rows = here * heads
    hist_rows = kg.shape[1]
    per_req = hist_rows // BLOCK
    blocks = per_req * REQS
    me = lax.axis_index("ctx")
    z, x = lax.div(me, 2), lax.rem(me, 2)

    def device(steps, cross):
        column = 1 - x if cross else x
        return {"ctx": lax.rem(z + (ring + steps) % ring, ring) * 2 + column}

    loads = [
        (q_in.at[:, pl.ds((g * heads + h) * HD, HD)], qbuf.at[0, g, OWN, pl.ds(h * here, here)])
        for g in (A, B)
        for h in range(heads)
    ]
    own_queries = len(loads)
    loads += [(owner_in, owner), (hist_in, hist)]
    loads += [(k_hbm, k_in), (v_hbm, v_in), (nk_in, nk), (nv_in, nv)]
    loads = [pltpu.make_async_copy(a, b, l_sem.at[i]) for i, (a, b) in enumerate(loads)]
    for load in loads:
        load.start()
    barrier = pltpu.get_barrier_semaphore()
    for partner in PARTNERS:
        pl.semaphore_signal(barrier, inc=1, device_id=device(*partner), device_id_type=MESH)
    for load in loads[:own_queries]:
        load.wait()
    pl.semaphore_wait(barrier, len(PARTNERS))

    def q_copy(n):
        p, g, c, steps, cross = QUERIES[n]
        d = (p - steps) % ring
        e = OTH if cross else c
        return pltpu.make_async_remote_copy(
            src_ref=qbuf.at[p, g, c],
            dst_ref=qbuf.at[d, g, e],
            send_sem=q_send.at[n],
            recv_sem=q_recv.at[d, g, e],
            device_id=device(steps, cross),
            device_id_type=MESH,
        )

    def q_wait(p, g, c):
        pltpu.make_async_remote_copy(
            src_ref=qbuf.at[p, g, c],
            dst_ref=qbuf.at[p, g, c],
            send_sem=q_send.at[0],
            recv_sem=q_recv.at[p, g, c],
            device_id=device(*PARTNERS[0]),
            device_id_type=MESH,
        ).wait_recv()

    def p_copies(n):
        p, g, c, steps, cross = MESSAGES[n]
        return [
            pltpu.make_async_remote_copy(
                src_ref=src.at[p, g, c],
                dst_ref=dst.at[n],
                send_sem=p_send.at[n, k],
                recv_sem=p_recv.at[n, k],
                device_id=device(steps, cross),
                device_id_type=MESH,
            )
            for k, (src, dst) in enumerate(((po, ro), (ps, rs)))
        ]

    def merged(parts):
        tops = [s[...] for _, s in parts]
        peak = functools.reduce(jnp.maximum, tops)
        weights = [jnp.exp2(t - peak) for t in tops]
        total = sum(weights[1:], weights[0])
        share = 1.0 / total
        acc = None
        for (o, _), w in zip(parts, weights):
            term = o[...].astype(jnp.float32) * (w * share)
            acc = term if acc is None else acc + term
        return acc, peak + jnp.log(total) * LOG2E

    def take(p, g, c, messages):
        parts = [(po.at[p, g, c], ps.at[p, g, c])]
        for message in messages:
            n = MESSAGES.index(message)
            for copy in p_copies(n):
                copy.wait_recv()
            parts.append((ro.at[n], rs.at[n]))
        return merged(parts)

    def finish(g):
        acc, _ = take(0, g, OWN, LAST[g])
        for h in range(heads):
            out[:, pl.ds((g * heads + h) * HD, HD)] = acc[:, h * here : (h + 1) * here].T

    def act(event):
        kind, *rest = event
        if kind == Q:
            q_copy(QUERIES.index(tuple(rest))).start()
        elif kind == S:
            for copy in p_copies(MESSAGES.index(tuple(rest))):
                copy.start()
        elif kind == F:
            p, g, c, messages = rest
            acc, lse = take(p, g, c, messages)
            po[p, g, c] = acc.astype(po.dtype)
            ps[p, g, c] = lse
        else:
            q_wait(*rest)

    arrived = {(0, A, OWN), (0, B, OWN)}

    def with_waits(events, unit):
        result = []
        needs = [(e, [e[1:4]] if e[0] == Q else []) for e in events]
        if unit < len(ORDER):
            needs.append((None, [ORDER[unit] + (c,) for c in (OWN, OTH)]))
        for event, blocks_of in needs:
            for block in blocks_of:
                if block not in arrived:
                    arrived.add(block)
                    result.append((None,) + block)
            if event is not None:
                result.append(event)
        return result

    none = len(ORDER)
    before = [with_waits(es, none) for es in BEFORE[:-2]]
    before += [with_waits(BEFORE[-2], 0), with_waits(BEFORE[-1], 1)]
    after = [with_waits(es, i + 2) for i, es in enumerate(AFTER)]

    for event in before[0]:
        act(event)
    for load in loads[own_queries:]:
        load.wait()

    lane = lax.broadcasted_iota(jnp.int32, (ONES, BLOCK), 1)
    sub = lax.broadcasted_iota(jnp.int32, (BLOCK, HD), 0)
    parts = len(before) - 3
    for i in range(blocks):
        r, b = i // per_req, i % per_req
        at, base = 0, 0
        for j in range(blocks):
            found = lax.div(owner[j], 2 * ring) == i
            at = jnp.where(found, j, at)
            base = jnp.where(found, owner[j], base)
        base = lax.rem(base, per_req * 2 * ring) * BLOCK
        keys = k_in[at]
        vals = v_in[at]
        if b == 0:
            first = keys
        left_over = hist[r] - base
        seen = sub < left_over
        kg[r, pl.ds(b * BLOCK, BLOCK), :] = jnp.where(seen, keys, first)
        vals = jnp.where(seen, vals, jnp.zeros_like(vals))
        vt[r, pl.ds(0, HD), pl.ds(b * BLOCK, BLOCK)] = vals.T
        vt[r, pl.ds(HD, ONES), pl.ds(b * BLOCK, BLOCK)] = jnp.where(
            lane < left_over, 1.0, 0.0
        ).astype(vt.dtype)
        if (i + 1) * parts % blocks == 0:
            for event in before[(i + 1) * parts // blocks]:
                act(event)
    vtn[pl.ds(0, HD), :] = nv[...].T
    vtn[pl.ds(HD, ONES), :] = jnp.ones((ONES, here), vtn.dtype)
    for event in before[-2]:
        act(event)

    step_p = [p for p, _ in ORDER]
    step_g = [g for _, g in ORDER]
    key_row = lax.broadcasted_iota(jnp.int32, (here, 2 * rows), 0)
    col = lax.broadcasted_iota(jnp.int32, (1, 2 * rows), 1)

    def place(i):
        if isinstance(i, int):
            return step_p[i], step_g[i]
        return table(step_p, i), table(step_g, i)

    def request_of(p):
        return lax.div(lax.rem(z + p, ring) * REQS, ring)

    def score(i, s):
        p, g = place(i)
        home = lax.rem(z + p, ring)
        r = request_of(p)
        q = qbuf[p, g].reshape(2 * rows, HD)
        s[pl.ds(0, hist_rows), :] = dot(kg[r], q, ((1,), (1,)))
        fresh = dot(nk[...], q, ((1,), (1,)))
        same = r == lax.div(z * REQS, ring)
        own_tok = jnp.where(same, (home * 2 + x) * here, -here)
        oth_tok = jnp.where(same, (home * 2 + 1 - x) * here, -here)
        query = jnp.where(col < rows, own_tok, oth_tok) + lax.rem(col, here)
        s[pl.ds(hist_rows, here), :] = jnp.where(me * here + key_row <= query, fresh, -1e30)

    def absorb(i, s):
        p, g = place(i)
        r = request_of(p)
        top = jnp.max(s[...], axis=0, keepdims=True) * SCALE
        probs = jnp.exp2(s[pl.ds(0, hist_rows), :] * SCALE - top).astype(jnp.bfloat16)
        fresh = jnp.exp2(s[pl.ds(hist_rows, here), :] * SCALE - top).astype(jnp.bfloat16)
        acc = dot(vt[r], probs, ((1,), (0,))) + dot(vtn[...], fresh, ((1,), (0,)))
        total = acc[HD : HD + 1]
        part = (acc[:HD] * (1.0 / total)).astype(po.dtype)
        lse = top + jnp.log(total) * LOG2E
        for c in (OWN, OTH):
            po[p, g, c] = part[:, c * rows : (c + 1) * rows]
            ps[p, g, c] = lse[:, c * rows : (c + 1) * rows]

    def react(h, half):
        for k in range(len(ORDER) // 2 - 1):
            if after[2 * k + half]:

                @pl.when(h == k)
                def _():
                    for event in after[2 * k + half]:
                        act(event)

    score(0, s0)
    for event in before[-1]:
        act(event)

    @pl.loop(0, len(ORDER) // 2 - 1)
    def _(h):
        score(2 * h + 1, s1)
        absorb(2 * h, s0)
        react(h, 0)
        score(2 * h + 2, s0)
        absorb(2 * h + 1, s1)
        react(h, 1)

    last = len(ORDER) - 1
    score(last, s1)
    absorb(last - 1, s0)
    for event in after[last - 1]:
        act(event)
    absorb(last, s1)
    for event in after[last] + after[last + 1]:
        act(event)
    finish(A)
    finish(B)
    for n in range(len(QUERIES)):
        q_copy(n).wait_send()
    for n in range(len(MESSAGES)):
        for copy in p_copies(n):
            copy.wait_send()


def local(queries, new_keys, new_values, cache_keys, cache_values, block_owner, history_len):
    here, width = queries.shape
    ring = lax.axis_size("ctx") // 2
    heads = width // HD
    rows = here * heads // 2
    slots = cache_keys.shape[0]
    hist_rows = slots // REQS
    bf, f32 = jnp.bfloat16, jnp.float32
    hbm = pl.BlockSpec(memory_space=pltpu.HBM)
    dma = pltpu.SemaphoreType.DMA
    all_rows = 4 * rows * ring
    keys = hist_rows + here
    return pl.pallas_call(
        functools.partial(kernel, ring),
        out_shape=pltpu.VMEM((here, width), f32),
        in_specs=[hbm] * 7,
        out_specs=pl.BlockSpec(memory_space=pltpu.VMEM),
        scratch_shapes=[
            pltpu.VMEM((ring, 2, 2, rows, HD), bf),
            pltpu.SMEM(block_owner.shape, jnp.int32),
            pltpu.SMEM(history_len.shape, jnp.int32),
            pltpu.VMEM((here, HD), bf),
            pltpu.VMEM((here, HD), bf),
            pltpu.VMEM((slots // BLOCK, BLOCK, HD), bf),
            pltpu.VMEM((slots // BLOCK, BLOCK, HD), bf),
            pltpu.VMEM((REQS, hist_rows, HD), bf),
            pltpu.VMEM((REQS, HD + ONES, hist_rows), bf),
            pltpu.VMEM((HD + ONES, here), bf),
            pltpu.VMEM((keys, 2 * rows), f32),
            pltpu.VMEM((keys, 2 * rows), f32),
            pltpu.VMEM((ring, 2, 2, HD, rows), bf),
            pltpu.VMEM((ring, 2, 2, 1, rows), f32),
            pltpu.VMEM((len(MESSAGES), HD, rows), bf),
            pltpu.VMEM((len(MESSAGES), 1, rows), f32),
            dma((heads + 6,)),
            dma((len(QUERIES),)),
            dma((ring, 2, 2)),
            dma((len(MESSAGES), 2)),
            dma((len(MESSAGES), 2)),
        ],
        compiler_params=pltpu.CompilerParams(
            collective_id=0, has_side_effects=True, vmem_limit_bytes=54 * 2**20 - 0 * 2**10
        ),
        cost_estimate=pl.CostEstimate(
            flops=4 * all_rows * keys * HD,
            bytes_accessed=4 * slots * HD + 6 * here * width,
            transcendentals=all_rows * keys,
        ),
    )(
        queries,
        new_keys,
        new_values,
        cache_keys.reshape(-1, BLOCK, HD),
        cache_values.reshape(-1, BLOCK, HD),
        block_owner,
        history_len,
    )


def solution(mesh):
    rows = P(("rep", "ctx"), "tp")
    return jax.shard_map(
        local,
        mesh=mesh,
        in_specs=(rows,) * 5 + (P(("rep", "ctx")), P("rep")),
        out_specs=rows,
        check_vma=False,
    )
```

```python
import functools
import math

import jax
import jax.numpy as jnp
from jax import lax
from jax.experimental import pallas as pl
from jax.experimental.pallas import tpu as pltpu
from jax.sharding import PartitionSpec as P

HD = 128
REQS = 2
BLOCK = 256
LOG2E = math.log2(math.e)
SCALE = LOG2E / math.sqrt(HD)
MESH = pl.DeviceIdType.MESH
A, B = 0, 1
OWN, OTH = 0, 1
ONES = 16
Q, S, F = 0, 1, 2

ORDER = (
    (1, 0),
    (0, 1),
    (7, 0),
    (7, 1),
    (2, 0),
    (6, 0),
    (1, 1),
    (3, 0),
    (5, 0),
    (5, 1),
    (4, 0),
    (4, 1),
    (3, 1),
    (2, 1),
    (6, 1),
    (0, 0),
)
BEFORE = (
    ((Q, 0, 0, 0, -1, 1), (Q, 0, 1, 0, 1, 0), (Q, 0, 0, 0, 1, 0), (Q, 0, 1, 0, 0, 1), (Q, 0, 0, 0, -1, 0), (Q, 0, 0, 0, 1, 1), (Q, 0, 1, 0, -1, 0), (Q, 0, 0, 0, 0, 1),),
    (),
    (),
    (),
    (),
    (),
    (),
    (),
    (),
    ((Q, 7, 1, 0, 1, 0), (Q, 7, 1, 0, 0, 1), (Q, 1, 0, 1, -1, 0), (Q, 1, 0, 0, -1, 0), (Q, 7, 0, 0, 1, 0),),
    (),
)
AFTER = (
    ((Q, 1, 1, 0, -1, 0), (Q, 1, 1, 0, 0, 1), (Q, 7, 0, 1, 1, 0),),
    ((Q, 6, 1, 0, 0, 1), (Q, 2, 0, 1, -1, 0), (Q, 6, 1, 0, 1, 0), (S, 0, 1, 1, 0, 1),),
    ((Q, 6, 0, 0, 1, 0), (Q, 2, 0, 0, -1, 0),),
    ((Q, 2, 1, 0, -2, 0), (Q, 2, 1, 0, 0, 1), (Q, 6, 0, 1, 1, 0), (Q, 2, 1, 0, -1, 0), (S, 7, 1, 1, 0, 1),),
    ((Q, 3, 0, 1, -1, 0), (Q, 5, 1, 0, 0, 1),),
    ((Q, 5, 0, 0, 1, 0),),
    ((Q, 4, 1, 0, 0, 1), (S, 1, 1, 1, 0, 1),),
    ((F, 7, 1, 0, ((7, 1, 1, 0, 1),)), (S, 7, 1, 0, -1, 0), (S, 3, 0, 0, 1, 0), (S, 3, 0, 1, 1, 0), (Q, 3, 1, 0, 0, 1),),
    ((S, 5, 0, 0, -1, 0), (S, 5, 0, 1, -1, 0),),
    ((S, 5, 1, 1, 0, 1),),
    ((S, 4, 0, 1, -2, 0), (S, 4, 0, 0, 2, 0), (F, 1, 1, 0, ((1, 1, 1, 0, 1),)), (S, 1, 1, 0, 1, 0),),
    ((F, 6, 0, 0, ((5, 0, 0, -1, 0),)), (S, 6, 0, 0, -1, 0), (F, 2, 0, 1, ((3, 0, 1, 1, 0),)), (S, 2, 0, 1, 1, 0), (S, 4, 1, 1, 0, 1),),
    ((S, 3, 1, 1, 0, 1), (F, 5, 1, 0, ((5, 1, 1, 0, 1),)), (S, 5, 1, 0, -1, 0),),
    ((F, 2, 0, 0, ((4, 0, 0, 2, 0), (3, 0, 0, 1, 0))), (S, 2, 0, 0, 1, 0), (S, 2, 1, 1, 0, 1), (F, 6, 0, 1, ((4, 0, 1, -2, 0), (5, 0, 1, -1, 0))), (S, 6, 0, 1, -1, 0),),
    ((S, 6, 1, 1, 0, 1), (F, 4, 1, 0, ((4, 1, 1, 0, 1),)), (S, 4, 1, 0, -2, 0), (F, 7, 0, 0, ((6, 0, 0, -1, 0),)), (S, 7, 0, 0, -1, 0),),
    ((F, 3, 1, 0, ((3, 1, 1, 0, 1),)), (S, 3, 1, 0, 1, 0), (S, 0, 0, 1, 0, 1), (F, 1, 0, 1, ((2, 0, 1, 1, 0),)), (S, 1, 0, 1, 1, 1),),
    ((F, 2, 1, 0, ((2, 1, 1, 0, 1),)), (F, 7, 0, 1, ((6, 0, 1, -1, 0),)), (S, 7, 0, 1, -1, 1), (F, 1, 0, 0, ((2, 0, 0, 1, 0),)), (S, 1, 0, 0, 1, 0), (F, 6, 1, 0, ((6, 1, 1, 0, 1),)), (F, 6, 1, 0, ((4, 1, 0, -2, 0), (5, 1, 0, -1, 0))), (S, 6, 1, 0, -2, 0), (F, 2, 1, 0, ((3, 1, 0, 1, 0),)), (S, 2, 1, 0, 2, 0),),
)
LAST = (
    ((1, 0, 0, 1, 0), (7, 0, 0, -1, 0), (1, 0, 1, 1, 1), (7, 0, 1, -1, 1), (0, 0, 1, 0, 1),),
    ((2, 1, 0, 2, 0), (1, 1, 0, 1, 0), (6, 1, 0, -2, 0), (7, 1, 0, -1, 0), (0, 1, 1, 0, 1),),
)

MESSAGES = tuple(e[1:] for es in BEFORE + AFTER for e in es if e[0] == S)
QUERIES = tuple(e[1:] for es in BEFORE + AFTER for e in es if e[0] == Q)
PARTNERS = tuple(sorted({m[3:] for m in MESSAGES + QUERIES}))


def dot(a, b, dims):
    return lax.dot_general(a, b, (dims, ((), ())), preferred_element_type=jnp.float32)


def table(values, index):
    out = values[0]
    for k, v in enumerate(values):
        if k:
            out = jnp.where(index == k, v, out)
    return out


def kernel(
    ring, q_in, nk_in, nv_in, k_hbm, v_hbm, owner_in, hist_in, out,
    qbuf, owner, hist, nk, nv, k_in, v_in, kg, vt, vtn, s0, s1, po, ps, ro, rs,
    l_sem, q_send, q_recv, p_send, p_recv,
):
    here, width = q_in.shape
    heads = width // HD // 2
    rows = here * heads
    hist_rows = kg.shape[1]
    per_req = hist_rows // BLOCK
    blocks = per_req * REQS
    me = lax.axis_index("ctx")
    z, x = lax.div(me, 2), lax.rem(me, 2)

    def device(steps, cross):
        column = 1 - x if cross else x
        return {"ctx": lax.rem(z + (ring + steps) % ring, ring) * 2 + column}

    loads = [
        (q_in.at[:, pl.ds((g * heads + h) * HD, HD)], qbuf.at[0, g, OWN, pl.ds(h * here, here)])
        for g in (A, B)
        for h in range(heads)
    ]
    own_queries = len(loads)
    loads += [(owner_in, owner), (hist_in, hist)]
    loads += [(k_hbm, k_in), (v_hbm, v_in), (nk_in, nk), (nv_in, nv)]
    loads = [pltpu.make_async_copy(a, b, l_sem.at[i]) for i, (a, b) in enumerate(loads)]
    for load in loads:
        load.start()
    barrier = pltpu.get_barrier_semaphore()
    for partner in PARTNERS:
        pl.semaphore_signal(barrier, inc=1, device_id=device(*partner), device_id_type=MESH)
    for load in loads[:own_queries]:
        load.wait()
    pl.semaphore_wait(barrier, len(PARTNERS))

    def q_copy(n):
        p, g, c, steps, cross = QUERIES[n]
        d = (p - steps) % ring
        e = OTH if cross else c
        return pltpu.make_async_remote_copy(
            src_ref=qbuf.at[p, g, c],
            dst_ref=qbuf.at[d, g, e],
            send_sem=q_send.at[n],
            recv_sem=q_recv.at[d, g, e],
            device_id=device(steps, cross),
            device_id_type=MESH,
        )

    def q_wait(p, g, c):
        pltpu.make_async_remote_copy(
            src_ref=qbuf.at[p, g, c],
            dst_ref=qbuf.at[p, g, c],
            send_sem=q_send.at[0],
            recv_sem=q_recv.at[p, g, c],
            device_id=device(*PARTNERS[0]),
            device_id_type=MESH,
        ).wait_recv()

    def p_copies(n):
        p, g, c, steps, cross = MESSAGES[n]
        return [
            pltpu.make_async_remote_copy(
                src_ref=src.at[p, g, c],
                dst_ref=dst.at[n],
                send_sem=p_send.at[n, k],
                recv_sem=p_recv.at[n, k],
                device_id=device(steps, cross),
                device_id_type=MESH,
            )
            for k, (src, dst) in enumerate(((po, ro), (ps, rs)))
        ]

    def merged(parts):
        tops = [s[...] for _, s in parts]
        peak = functools.reduce(jnp.maximum, tops)
        weights = [jnp.exp2(t - peak) for t in tops]
        total = sum(weights[1:], weights[0])
        share = 1.0 / total
        acc = None
        for (o, _), w in zip(parts, weights):
            term = o[...].astype(jnp.float32) * (w * share)
            acc = term if acc is None else acc + term
        return acc, peak + jnp.log(total) * LOG2E

    def take(p, g, c, messages):
        parts = [(po.at[p, g, c], ps.at[p, g, c])]
        for message in messages:
            n = MESSAGES.index(message)
            for copy in p_copies(n):
                copy.wait_recv()
            parts.append((ro.at[n], rs.at[n]))
        return merged(parts)

    def finish(g):
        acc, _ = take(0, g, OWN, LAST[g])
        for h in range(heads):
            out[:, pl.ds((g * heads + h) * HD, HD)] = acc[:, h * here : (h + 1) * here].T

    def act(event):
        kind, *rest = event
        if kind == Q:
            q_copy(QUERIES.index(tuple(rest))).start()
        elif kind == S:
            for copy in p_copies(MESSAGES.index(tuple(rest))):
                copy.start()
        elif kind == F:
            p, g, c, messages = rest
            acc, lse = take(p, g, c, messages)
            po[p, g, c] = acc.astype(po.dtype)
            ps[p, g, c] = lse
        else:
            q_wait(*rest)

    arrived = {(0, A, OWN), (0, B, OWN)}

    def with_waits(events, unit):
        result = []
        needs = [(e, [e[1:4]] if e[0] == Q else []) for e in events]
        if unit < len(ORDER):
            needs.append((None, [ORDER[unit] + (c,) for c in (OWN, OTH)]))
        for event, blocks_of in needs:
            for block in blocks_of:
                if block not in arrived:
                    arrived.add(block)
                    result.append((None,) + block)
            if event is not None:
                result.append(event)
        return result

    none = len(ORDER)
    before = [with_waits(es, none) for es in BEFORE[:-2]]
    before += [with_waits(BEFORE[-2], 0), with_waits(BEFORE[-1], 1)]
    after = [with_waits(es, i + 2) for i, es in enumerate(AFTER)]

    for event in before[0]:
        act(event)
    for load in loads[own_queries:]:
        load.wait()

    lane = lax.broadcasted_iota(jnp.int32, (ONES, BLOCK), 1)
    sub = lax.broadcasted_iota(jnp.int32, (BLOCK, HD), 0)
    parts = len(before) - 3
    for i in range(blocks):
        r, b = i // per_req, i % per_req
        at, base = 0, 0
        for j in range(blocks):
            found = lax.div(owner[j], 2 * ring) == i
            at = jnp.where(found, j, at)
            base = jnp.where(found, owner[j], base)
        base = lax.rem(base, per_req * 2 * ring) * BLOCK
        keys = k_in[at]
        vals = v_in[at]
        if b == 0:
            first = keys
        left_over = hist[r] - base
        seen = sub < left_over
        kg[r, pl.ds(b * BLOCK, BLOCK), :] = jnp.where(seen, keys, first)
        vals = jnp.where(seen, vals, jnp.zeros_like(vals))
        vt[r, pl.ds(0, HD), pl.ds(b * BLOCK, BLOCK)] = vals.T
        vt[r, pl.ds(HD, ONES), pl.ds(b * BLOCK, BLOCK)] = jnp.where(
            lane < left_over, 1.0, 0.0
        ).astype(vt.dtype)
        if (i + 1) * parts % blocks == 0:
            for event in before[(i + 1) * parts // blocks]:
                act(event)
    vtn[pl.ds(0, HD), :] = nv[...].T
    vtn[pl.ds(HD, ONES), :] = jnp.ones((ONES, here), vtn.dtype)
    for event in before[-2]:
        act(event)

    step_p = [p for p, _ in ORDER]
    step_g = [g for _, g in ORDER]
    key_row = lax.broadcasted_iota(jnp.int32, (here, 2 * rows), 0)
    col = lax.broadcasted_iota(jnp.int32, (1, 2 * rows), 1)

    def place(i):
        if isinstance(i, int):
            return step_p[i], step_g[i]
        return table(step_p, i), table(step_g, i)

    def request_of(p):
        return lax.div(lax.rem(z + p, ring) * REQS, ring)

    def score(i, s):
        p, g = place(i)
        home = lax.rem(z + p, ring)
        r = request_of(p)
        q = qbuf[p, g].reshape(2 * rows, HD)
        s[pl.ds(0, hist_rows), :] = dot(kg[r], q, ((1,), (1,)))
        fresh = dot(nk[...], q, ((1,), (1,)))
        same = r == lax.div(z * REQS, ring)
        own_tok = jnp.where(same, (home * 2 + x) * here, -here)
        oth_tok = jnp.where(same, (home * 2 + 1 - x) * here, -here)
        query = jnp.where(col < rows, own_tok, oth_tok) + lax.rem(col, here)
        s[pl.ds(hist_rows, here), :] = jnp.where(me * here + key_row <= query, fresh, -1e30)

    def absorb(i, s):
        p, g = place(i)
        r = request_of(p)
        top = jnp.max(s[...], axis=0, keepdims=True) * SCALE
        probs = jnp.exp2(s[pl.ds(0, hist_rows), :] * SCALE - top).astype(jnp.bfloat16)
        fresh = jnp.exp2(s[pl.ds(hist_rows, here), :] * SCALE - top).astype(jnp.bfloat16)
        acc = dot(vt[r], probs, ((1,), (0,))) + dot(vtn[...], fresh, ((1,), (0,)))
        total = acc[HD : HD + 1]
        part = (acc[:HD] * (1.0 / total)).astype(po.dtype)
        lse = top + jnp.log(total) * LOG2E
        for c in (OWN, OTH):
            po[p, g, c] = part[:, c * rows : (c + 1) * rows]
            ps[p, g, c] = lse[:, c * rows : (c + 1) * rows]

    def react(h, half):
        for k in range(len(ORDER) // 2 - 1):
            if after[2 * k + half]:

                @pl.when(h == k)
                def _():
                    for event in after[2 * k + half]:
                        act(event)

    score(0, s0)
    for event in before[-1]:
        act(event)

    @pl.loop(0, len(ORDER) // 2 - 1)
    def _(h):
        score(2 * h + 1, s1)
        absorb(2 * h, s0)
        react(h, 0)
        score(2 * h + 2, s0)
        absorb(2 * h + 1, s1)
        react(h, 1)

    last = len(ORDER) - 1
    score(last, s1)
    absorb(last - 1, s0)
    for event in after[last - 1]:
        act(event)
    absorb(last, s1)
    for event in after[last] + after[last + 1]:
        act(event)
    finish(A)
    finish(B)
    for n in range(len(QUERIES)):
        q_copy(n).wait_send()
    for n in range(len(MESSAGES)):
        for copy in p_copies(n):
            copy.wait_send()


def local(queries, new_keys, new_values, cache_keys, cache_values, block_owner, history_len):
    here, width = queries.shape
    ring = lax.axis_size("ctx") // 2
    heads = width // HD
    rows = here * heads // 2
    slots = cache_keys.shape[0]
    hist_rows = slots // REQS
    bf, f32 = jnp.bfloat16, jnp.float32
    hbm = pl.BlockSpec(memory_space=pltpu.HBM)
    dma = pltpu.SemaphoreType.DMA
    all_rows = 4 * rows * ring
    keys = hist_rows + here
    return pl.pallas_call(
        functools.partial(kernel, ring),
        out_shape=pltpu.VMEM((here, width), f32),
        in_specs=[hbm] * 7,
        out_specs=pl.BlockSpec(memory_space=pltpu.VMEM),
        scratch_shapes=[
            pltpu.VMEM((ring, 2, 2, rows, HD), bf),
            pltpu.SMEM(block_owner.shape, jnp.int32),
            pltpu.SMEM(history_len.shape, jnp.int32),
            pltpu.VMEM((here, HD), bf),
            pltpu.VMEM((here, HD), bf),
            pltpu.VMEM((slots // BLOCK, BLOCK, HD), bf),
            pltpu.VMEM((slots // BLOCK, BLOCK, HD), bf),
            pltpu.VMEM((REQS, hist_rows, HD), bf),
            pltpu.VMEM((REQS, HD + ONES, hist_rows), bf),
            pltpu.VMEM((HD + ONES, here), bf),
            pltpu.VMEM((keys, 2 * rows), f32),
            pltpu.VMEM((keys, 2 * rows), f32),
            pltpu.VMEM((ring, 2, 2, HD, rows), bf),
            pltpu.VMEM((ring, 2, 2, 1, rows), f32),
            pltpu.VMEM((len(MESSAGES), HD, rows), bf),
            pltpu.VMEM((len(MESSAGES), 1, rows), f32),
            dma((heads + 6,)),
            dma((len(QUERIES),)),
            dma((ring, 2, 2)),
            dma((len(MESSAGES), 2)),
            dma((len(MESSAGES), 2)),
        ],
        compiler_params=pltpu.CompilerParams(
            collective_id=0, has_side_effects=True, vmem_limit_bytes=54 * 2**20
        ),
        cost_estimate=pl.CostEstimate(
            flops=4 * all_rows * keys * HD,
            bytes_accessed=4 * slots * HD + 6 * here * width,
            transcendentals=all_rows * keys,
        ),
    )(
        queries,
        new_keys,
        new_values,
        cache_keys.reshape(-1, BLOCK, HD),
        cache_values.reshape(-1, BLOCK, HD),
        block_owner,
        history_len,
    )


def solution(mesh):
    rows = P(("rep", "ctx"), "tp")
    return jax.shard_map(
        local,
        mesh=mesh,
        in_specs=(rows,) * 5 + (P(("rep", "ctx")), P("rep")),
        out_specs=rows,
        check_vma=False,
    )
```

```python
import functools
import math

import jax
import jax.numpy as jnp
from jax import lax
from jax.experimental import pallas as pl
from jax.experimental.pallas import tpu as pltpu
from jax.sharding import PartitionSpec as P

HD = 128
REQS = 2
BLOCK = 256
LOG2E = math.log2(math.e)
SCALE = LOG2E / math.sqrt(HD)
MESH = pl.DeviceIdType.MESH
A, B = 0, 1
OWN, OTH = 0, 1
ONES = 16
Q, S, F = 0, 1, 2

ORDER = (
    (1, 0),
    (0, 1),
    (7, 0),
    (7, 1),
    (2, 0),
    (6, 0),
    (1, 1),
    (3, 0),
    (5, 0),
    (5, 1),
    (4, 0),
    (4, 1),
    (3, 1),
    (2, 1),
    (6, 1),
    (0, 0),
)
BEFORE = (
    ((Q, 0, 0, 0, -1, 1), (Q, 0, 1, 0, 1, 0), (Q, 0, 0, 0, 1, 0), (Q, 0, 1, 0, 0, 1), (Q, 0, 0, 0, -1, 0), (Q, 0, 0, 0, 1, 1), (Q, 0, 1, 0, -1, 0), (Q, 0, 0, 0, 0, 1),),
    (),
    (),
    (),
    (),
    (),
    (),
    (),
    (),
    ((Q, 7, 1, 0, 1, 0), (Q, 7, 1, 0, 0, 1), (Q, 1, 0, 1, -1, 0), (Q, 1, 0, 0, -1, 0), (Q, 7, 0, 0, 1, 0),),
    (),
)
AFTER = (
    ((Q, 1, 1, 0, -1, 0), (Q, 1, 1, 0, 0, 1), (Q, 7, 0, 1, 1, 0),),
    ((Q, 6, 1, 0, 0, 1), (Q, 2, 0, 1, -1, 0), (Q, 6, 1, 0, 1, 0), (S, 0, 1, 1, 0, 1),),
    ((Q, 6, 0, 0, 1, 0), (Q, 2, 0, 0, -1, 0),),
    ((Q, 2, 1, 0, -2, 0), (Q, 2, 1, 0, 0, 1), (Q, 6, 0, 1, 1, 0), (Q, 2, 1, 0, -1, 0), (S, 7, 1, 1, 0, 1),),
    ((Q, 3, 0, 1, -1, 0), (Q, 5, 1, 0, 0, 1),),
    ((Q, 5, 0, 0, 1, 0),),
    ((Q, 4, 1, 0, 0, 1), (S, 1, 1, 1, 0, 1),),
    ((F, 7, 1, 0, ((7, 1, 1, 0, 1),)), (S, 7, 1, 0, -1, 0), (S, 3, 0, 0, 1, 0), (S, 3, 0, 1, 1, 0), (Q, 3, 1, 0, 0, 1),),
    ((S, 5, 0, 0, -1, 0), (S, 5, 0, 1, -1, 0),),
    ((S, 5, 1, 1, 0, 1),),
    ((S, 4, 0, 1, -2, 0), (S, 4, 0, 0, 2, 0), (F, 1, 1, 0, ((1, 1, 1, 0, 1),)), (S, 1, 1, 0, 1, 0),),
    ((F, 6, 0, 0, ((5, 0, 0, -1, 0),)), (S, 6, 0, 0, -1, 0), (F, 2, 0, 1, ((3, 0, 1, 1, 0),)), (S, 2, 0, 1, 1, 0), (S, 4, 1, 1, 0, 1),),
    ((S, 3, 1, 1, 0, 1), (F, 5, 1, 0, ((5, 1, 1, 0, 1),)), (S, 5, 1, 0, -1, 0),),
    ((F, 2, 0, 0, ((4, 0, 0, 2, 0), (3, 0, 0, 1, 0))), (S, 2, 0, 0, 1, 0), (S, 2, 1, 1, 0, 1), (F, 6, 0, 1, ((4, 0, 1, -2, 0), (5, 0, 1, -1, 0))), (S, 6, 0, 1, -1, 0),),
    ((S, 6, 1, 1, 0, 1), (F, 4, 1, 0, ((4, 1, 1, 0, 1),)), (S, 4, 1, 0, -2, 0), (F, 7, 0, 0, ((6, 0, 0, -1, 0),)), (S, 7, 0, 0, -1, 0),),
    ((F, 3, 1, 0, ((3, 1, 1, 0, 1),)), (S, 3, 1, 0, 1, 0), (S, 0, 0, 1, 0, 1), (F, 1, 0, 1, ((2, 0, 1, 1, 0),)), (S, 1, 0, 1, 1, 1),),
    ((F, 2, 1, 0, ((2, 1, 1, 0, 1),)), (F, 7, 0, 1, ((6, 0, 1, -1, 0),)), (S, 7, 0, 1, -1, 1), (F, 1, 0, 0, ((2, 0, 0, 1, 0),)), (S, 1, 0, 0, 1, 0), (F, 6, 1, 0, ((6, 1, 1, 0, 1),)), (F, 6, 1, 0, ((4, 1, 0, -2, 0), (5, 1, 0, -1, 0))), (S, 6, 1, 0, -2, 0), (F, 2, 1, 0, ((3, 1, 0, 1, 0),)), (S, 2, 1, 0, 2, 0),),
)
LAST = (
    ((1, 0, 0, 1, 0), (7, 0, 0, -1, 0), (1, 0, 1, 1, 1), (7, 0, 1, -1, 1), (0, 0, 1, 0, 1),),
    ((2, 1, 0, 2, 0), (1, 1, 0, 1, 0), (6, 1, 0, -2, 0), (7, 1, 0, -1, 0), (0, 1, 1, 0, 1),),
)

MESSAGES = tuple(e[1:] for es in BEFORE + AFTER for e in es if e[0] == S)
QUERIES = tuple(e[1:] for es in BEFORE + AFTER for e in es if e[0] == Q)
PARTNERS = tuple(sorted({m[3:] for m in MESSAGES + QUERIES}))


def dot(a, b, dims):
    return lax.dot_general(a, b, (dims, ((), ())), preferred_element_type=jnp.float32)


def table(values, index):
    out = values[0]
    for k, v in enumerate(values):
        if k:
            out = jnp.where(index == k, v, out)
    return out


def kernel(
    ring, q_in, nk_in, nv_in, k_hbm, v_hbm, owner_in, hist_in, out,
    qbuf, owner, hist, nk, nv, k_in, v_in, kg, vt, vtn, s0, s1, po, ps, ro, rs,
    l_sem, q_send, q_recv, p_send, p_recv,
):
    here, width = q_in.shape
    heads = width // HD // 2
    rows = here * heads
    hist_rows = kg.shape[1]
    per_req = hist_rows // BLOCK
    blocks = per_req * REQS
    me = lax.axis_index("ctx")
    z, x = lax.div(me, 2), lax.rem(me, 2)

    def device(steps, cross):
        column = 1 - x if cross else x
        return {"ctx": lax.rem(z + (ring + steps) % ring, ring) * 2 + column}

    loads = [
        (q_in.at[:, pl.ds((g * heads + h) * HD, HD)], qbuf.at[0, g, OWN, pl.ds(h * here, here)])
        for g in (A, B)
        for h in range(heads)
    ]
    own_queries = len(loads)
    loads += [(owner_in, owner), (hist_in, hist)]
    loads += [(k_hbm, k_in), (v_hbm, v_in), (nk_in, nk), (nv_in, nv)]
    loads = [pltpu.make_async_copy(a, b, l_sem.at[i]) for i, (a, b) in enumerate(loads)]
    for load in loads:
        load.start()
    barrier = pltpu.get_barrier_semaphore()
    for partner in PARTNERS:
        pl.semaphore_signal(barrier, inc=1, device_id=device(*partner), device_id_type=MESH)
    for load in loads[:own_queries]:
        load.wait()
    pl.semaphore_wait(barrier, len(PARTNERS))

    def q_copy(n):
        p, g, c, steps, cross = QUERIES[n]
        d = (p - steps) % ring
        e = OTH if cross else c
        return pltpu.make_async_remote_copy(
            src_ref=qbuf.at[p, g, c],
            dst_ref=qbuf.at[d, g, e],
            send_sem=q_send.at[n],
            recv_sem=q_recv.at[d, g, e],
            device_id=device(steps, cross),
            device_id_type=MESH,
        )

    def q_wait(p, g, c):
        pltpu.make_async_remote_copy(
            src_ref=qbuf.at[p, g, c],
            dst_ref=qbuf.at[p, g, c],
            send_sem=q_send.at[0],
            recv_sem=q_recv.at[p, g, c],
            device_id=device(*PARTNERS[0]),
            device_id_type=MESH,
        ).wait_recv()

    def p_copies(n):
        p, g, c, steps, cross = MESSAGES[n]
        return [
            pltpu.make_async_remote_copy(
                src_ref=src.at[p, g, c],
                dst_ref=dst.at[n],
                send_sem=p_send.at[n, k],
                recv_sem=p_recv.at[n, k],
                device_id=device(steps, cross),
                device_id_type=MESH,
            )
            for k, (src, dst) in enumerate(((po, ro), (ps, rs)))
        ]

    def merged(parts):
        tops = [s[...] for _, s in parts]
        peak = functools.reduce(jnp.maximum, tops)
        weights = [jnp.exp2(t - peak) for t in tops]
        total = sum(weights[1:], weights[0])
        share = 1.0 / total
        acc = None
        for (o, _), w in zip(parts, weights):
            term = o[...].astype(jnp.float32) * (w * share)
            acc = term if acc is None else acc + term
        return acc, peak + jnp.log(total) * LOG2E

    def take(p, g, c, messages):
        parts = [(po.at[p, g, c], ps.at[p, g, c])]
        for message in messages:
            n = MESSAGES.index(message)
            for copy in p_copies(n):
                copy.wait_recv()
            parts.append((ro.at[n], rs.at[n]))
        return merged(parts)

    def finish(g):
        acc, _ = take(0, g, OWN, LAST[g])
        for h in range(heads):
            out[:, pl.ds((g * heads + h) * HD, HD)] = acc[:, h * here : (h + 1) * here].T

    def act(event):
        kind, *rest = event
        if kind == Q:
            q_copy(QUERIES.index(tuple(rest))).start()
        elif kind == S:
            for copy in p_copies(MESSAGES.index(tuple(rest))):
                copy.start()
        elif kind == F:
            p, g, c, messages = rest
            acc, lse = take(p, g, c, messages)
            po[p, g, c] = acc.astype(po.dtype)
            ps[p, g, c] = lse
        else:
            q_wait(*rest)

    arrived = {(0, A, OWN), (0, B, OWN)}

    def with_waits(events, unit):
        result = []
        needs = [(e, [e[1:4]] if e[0] == Q else []) for e in events]
        if unit < len(ORDER):
            needs.append((None, [ORDER[unit] + (c,) for c in (OWN, OTH)]))
        for event, blocks_of in needs:
            for block in blocks_of:
                if block not in arrived:
                    arrived.add(block)
                    result.append((None,) + block)
            if event is not None:
                result.append(event)
        return result

    none = len(ORDER)
    before = [with_waits(es, none) for es in BEFORE[:-2]]
    before += [with_waits(BEFORE[-2], 0), with_waits(BEFORE[-1], 1)]
    after = [with_waits(es, i + 2) for i, es in enumerate(AFTER)]

    for event in before[0]:
        act(event)
    for load in loads[own_queries:]:
        load.wait()

    lane = lax.broadcasted_iota(jnp.int32, (ONES, BLOCK), 1)
    sub = lax.broadcasted_iota(jnp.int32, (BLOCK, HD), 0)
    parts = len(before) - 3
    for i in range(blocks):
        r, b = i // per_req, i % per_req
        at, base = 0, 0
        for j in range(blocks):
            found = lax.div(owner[j], 2 * ring) == i
            at = jnp.where(found, j, at)
            base = jnp.where(found, owner[j], base)
        base = lax.rem(base, per_req * 2 * ring) * BLOCK
        keys = k_in[at]
        vals = v_in[at]
        if b == 0:
            first = keys
        left_over = hist[r] - base
        seen = sub < left_over
        kg[r, pl.ds(b * BLOCK, BLOCK), :] = jnp.where(seen, keys, first)
        vals = jnp.where(seen, vals, jnp.zeros_like(vals))
        vt[r, pl.ds(0, HD), pl.ds(b * BLOCK, BLOCK)] = vals.T
        vt[r, pl.ds(HD, ONES), pl.ds(b * BLOCK, BLOCK)] = jnp.where(
            lane < left_over, 1.0, 0.0
        ).astype(vt.dtype)
        if (i + 1) * parts % blocks == 0:
            for event in before[(i + 1) * parts // blocks]:
                act(event)
    vtn[pl.ds(0, HD), :] = nv[...].T
    vtn[pl.ds(HD, ONES), :] = jnp.ones((ONES, here), vtn.dtype)
    for event in before[-2]:
        act(event)

    step_p = [p for p, _ in ORDER]
    step_g = [g for _, g in ORDER]
    key_row = lax.broadcasted_iota(jnp.int32, (here, 2 * rows), 0)
    col = lax.broadcasted_iota(jnp.int32, (1, 2 * rows), 1)

    def place(i):
        if isinstance(i, int):
            return step_p[i], step_g[i]
        return table(step_p, i), table(step_g, i)

    def request_of(p):
        return lax.div(lax.rem(z + p, ring) * REQS, ring)

    def score(i, s):
        p, g = place(i)
        home = lax.rem(z + p, ring)
        r = request_of(p)
        q = qbuf[p, g].reshape(2 * rows, HD)
        s[pl.ds(0, hist_rows), :] = dot(kg[r], q, ((1,), (1,)))
        fresh = dot(nk[...], q, ((1,), (1,)))
        same = r == lax.div(z * REQS, ring)
        own_tok = jnp.where(same, (home * 2 + x) * here, -here)
        oth_tok = jnp.where(same, (home * 2 + 1 - x) * here, -here)
        query = jnp.where(col < rows, own_tok, oth_tok) + lax.rem(col, here)
        s[pl.ds(hist_rows, here), :] = jnp.where(me * here + key_row <= query, fresh, -1e30)

    def absorb(i, s):
        p, g = place(i)
        r = request_of(p)
        top = jnp.max(s[...], axis=0, keepdims=True) * SCALE
        probs = jnp.exp2(s[pl.ds(0, hist_rows), :] * SCALE - top).astype(jnp.bfloat16)
        fresh = jnp.exp2(s[pl.ds(hist_rows, here), :] * SCALE - top).astype(jnp.bfloat16)
        acc = dot(vt[r], probs, ((1,), (0,))) + dot(vtn[...], fresh, ((1,), (0,)))
        total = acc[HD : HD + 1]
        part = (acc[:HD] * (1.0 / total)).astype(po.dtype)
        lse = top + jnp.log(total) * LOG2E
        for c in (OWN, OTH):
            po[p, g, c] = part[:, c * rows : (c + 1) * rows]
            ps[p, g, c] = lse[:, c * rows : (c + 1) * rows]

    def react(h, half):
        for k in range(len(ORDER) // 2 - 1):
            if after[2 * k + half]:

                @pl.when(h == k)
                def _():
                    for event in after[2 * k + half]:
                        act(event)

    score(0, s0)
    for event in before[-1]:
        act(event)

    @pl.loop(0, len(ORDER) // 2 - 1)
    def _(h):
        score(2 * h + 1, s1)
        absorb(2 * h, s0)
        react(h, 0)
        score(2 * h + 2, s0)
        absorb(2 * h + 1, s1)
        react(h, 1)

    last = len(ORDER) - 1
    score(last, s1)
    absorb(last - 1, s0)
    for event in after[last - 1]:
        act(event)
    absorb(last, s1)
    for event in after[last] + after[last + 1]:
        act(event)
    for n in range(len(QUERIES)):
        q_copy(n).wait_send()
    for n in range(len(MESSAGES)):
        for copy in p_copies(n):
            copy.wait_send()
    finish(A)
    finish(B)


def local(queries, new_keys, new_values, cache_keys, cache_values, block_owner, history_len):
    here, width = queries.shape
    ring = lax.axis_size("ctx") // 2
    heads = width // HD
    rows = here * heads // 2
    slots = cache_keys.shape[0]
    hist_rows = slots // REQS
    bf, f32 = jnp.bfloat16, jnp.float32
    hbm = pl.BlockSpec(memory_space=pltpu.HBM)
    dma = pltpu.SemaphoreType.DMA
    all_rows = 4 * rows * ring
    keys = hist_rows + here
    return pl.pallas_call(
        functools.partial(kernel, ring),
        out_shape=pltpu.VMEM((here, width), f32),
        in_specs=[hbm] * 7,
        out_specs=pl.BlockSpec(memory_space=pltpu.VMEM),
        scratch_shapes=[
            pltpu.VMEM((ring, 2, 2, rows, HD), bf),
            pltpu.SMEM(block_owner.shape, jnp.int32),
            pltpu.SMEM(history_len.shape, jnp.int32),
            pltpu.VMEM((here, HD), bf),
            pltpu.VMEM((here, HD), bf),
            pltpu.VMEM((slots // BLOCK, BLOCK, HD), bf),
            pltpu.VMEM((slots // BLOCK, BLOCK, HD), bf),
            pltpu.VMEM((REQS, hist_rows, HD), bf),
            pltpu.VMEM((REQS, HD + ONES, hist_rows), bf),
            pltpu.VMEM((HD + ONES, here), bf),
            pltpu.VMEM((keys, 2 * rows), f32),
            pltpu.VMEM((keys, 2 * rows), f32),
            pltpu.VMEM((ring, 2, 2, HD, rows), bf),
            pltpu.VMEM((ring, 2, 2, 1, rows), f32),
            pltpu.VMEM((len(MESSAGES), HD, rows), bf),
            pltpu.VMEM((len(MESSAGES), 1, rows), f32),
            dma((heads + 6,)),
            dma((len(QUERIES),)),
            dma((ring, 2, 2)),
            dma((len(MESSAGES), 2)),
            dma((len(MESSAGES), 2)),
        ],
        compiler_params=pltpu.CompilerParams(
            collective_id=0, has_side_effects=True, vmem_limit_bytes=54 * 2**20
        ),
        cost_estimate=pl.CostEstimate(
            flops=4 * all_rows * keys * HD,
            bytes_accessed=4 * slots * HD + 6 * here * width,
            transcendentals=all_rows * keys,
        ),
    )(
        queries,
        new_keys,
        new_values,
        cache_keys.reshape(-1, BLOCK, HD),
        cache_values.reshape(-1, BLOCK, HD),
        block_owner,
        history_len,
    )


def solution(mesh):
    rows = P(("rep", "ctx"), "tp")
    return jax.shard_map(
        local,
        mesh=mesh,
        in_specs=(rows,) * 5 + (P(("rep", "ctx")), P("rep")),
        out_specs=rows,
        check_vma=False,
    )
```

```python
import functools
import math

import jax
import jax.numpy as jnp
from jax import lax
from jax.experimental import pallas as pl
from jax.experimental.pallas import tpu as pltpu
from jax.sharding import PartitionSpec as P

HD = 128
REQS = 2
BLOCK = 256
LOG2E = math.log2(math.e)
SCALE = LOG2E / math.sqrt(HD)
MESH = pl.DeviceIdType.MESH
A, B = 0, 1
OWN, OTH = 0, 1
ONES = 16
Q, S, F = 0, 1, 2

ORDER = (
    (1, 0),
    (0, 1),
    (7, 0),
    (7, 1),
    (2, 0),
    (6, 0),
    (1, 1),
    (3, 0),
    (5, 0),
    (5, 1),
    (4, 0),
    (4, 1),
    (3, 1),
    (2, 1),
    (6, 1),
    (0, 0),
)
BEFORE = (
    ((Q, 0, 0, 0, -1, 1), (Q, 0, 1, 0, 1, 0), (Q, 0, 0, 0, 1, 0), (Q, 0, 1, 0, 0, 1), (Q, 0, 0, 0, -1, 0), (Q, 0, 0, 0, 1, 1), (Q, 0, 1, 0, -1, 0), (Q, 0, 0, 0, 0, 1),),
    (),
    (),
    (),
    (),
    (),
    (),
    (),
    (),
    ((Q, 7, 1, 0, 1, 0), (Q, 7, 1, 0, 0, 1), (Q, 1, 0, 1, -1, 0), (Q, 1, 0, 0, -1, 0), (Q, 7, 0, 0, 1, 0),),
    (),
)
AFTER = (
    ((Q, 1, 1, 0, -1, 0), (Q, 1, 1, 0, 0, 1), (Q, 7, 0, 1, 1, 0),),
    ((Q, 6, 1, 0, 0, 1), (Q, 2, 0, 1, -1, 0), (Q, 6, 1, 0, 1, 0), (S, 0, 1, 1, 0, 1),),
    ((Q, 6, 0, 0, 1, 0), (Q, 2, 0, 0, -1, 0),),
    ((Q, 2, 1, 0, -2, 0), (Q, 2, 1, 0, 0, 1), (Q, 6, 0, 1, 1, 0), (Q, 2, 1, 0, -1, 0), (S, 7, 1, 1, 0, 1),),
    ((Q, 3, 0, 1, -1, 0), (Q, 5, 1, 0, 0, 1),),
    ((Q, 5, 0, 0, 1, 0),),
    ((Q, 4, 1, 0, 0, 1), (S, 1, 1, 1, 0, 1),),
    ((F, 7, 1, 0, ((7, 1, 1, 0, 1),)), (S, 7, 1, 0, -1, 0), (S, 3, 0, 0, 1, 0), (S, 3, 0, 1, 1, 0), (Q, 3, 1, 0, 0, 1),),
    ((S, 5, 0, 0, -1, 0), (S, 5, 0, 1, -1, 0),),
    ((S, 5, 1, 1, 0, 1),),
    ((S, 4, 0, 1, -2, 0), (S, 4, 0, 0, 2, 0), (F, 1, 1, 0, ((1, 1, 1, 0, 1),)), (S, 1, 1, 0, 1, 0),),
    ((F, 6, 0, 0, ((5, 0, 0, -1, 0),)), (S, 6, 0, 0, -1, 0), (F, 2, 0, 1, ((3, 0, 1, 1, 0),)), (S, 2, 0, 1, 1, 0), (S, 4, 1, 1, 0, 1),),
    ((S, 3, 1, 1, 0, 1), (F, 5, 1, 0, ((5, 1, 1, 0, 1),)), (S, 5, 1, 0, -1, 0),),
    ((F, 2, 0, 0, ((4, 0, 0, 2, 0), (3, 0, 0, 1, 0))), (S, 2, 0, 0, 1, 0), (S, 2, 1, 1, 0, 1), (F, 6, 0, 1, ((4, 0, 1, -2, 0), (5, 0, 1, -1, 0))), (S, 6, 0, 1, -1, 0),),
    ((S, 6, 1, 1, 0, 1), (F, 4, 1, 0, ((4, 1, 1, 0, 1),)), (S, 4, 1, 0, -2, 0), (F, 7, 0, 0, ((6, 0, 0, -1, 0),)), (S, 7, 0, 0, -1, 0),),
    ((F, 3, 1, 0, ((3, 1, 1, 0, 1),)), (S, 3, 1, 0, 1, 0), (S, 0, 0, 1, 0, 1), (F, 1, 0, 1, ((2, 0, 1, 1, 0),)), (S, 1, 0, 1, 1, 1),),
    ((F, 2, 1, 0, ((2, 1, 1, 0, 1),)), (F, 7, 0, 1, ((6, 0, 1, -1, 0),)), (S, 7, 0, 1, -1, 1), (F, 1, 0, 0, ((2, 0, 0, 1, 0),)), (S, 1, 0, 0, 1, 0), (F, 6, 1, 0, ((6, 1, 1, 0, 1),)), (F, 6, 1, 0, ((4, 1, 0, -2, 0), (5, 1, 0, -1, 0))), (S, 6, 1, 0, -2, 0), (F, 2, 1, 0, ((3, 1, 0, 1, 0),)), (S, 2, 1, 0, 2, 0),),
)
LAST = (
    ((1, 0, 0, 1, 0), (7, 0, 0, -1, 0), (1, 0, 1, 1, 1), (7, 0, 1, -1, 1), (0, 0, 1, 0, 1),),
    ((2, 1, 0, 2, 0), (1, 1, 0, 1, 0), (6, 1, 0, -2, 0), (7, 1, 0, -1, 0), (0, 1, 1, 0, 1),),
)

MESSAGES = tuple(e[1:] for es in BEFORE + AFTER for e in es if e[0] == S)
QUERIES = tuple(e[1:] for es in BEFORE + AFTER for e in es if e[0] == Q)
PARTNERS = tuple(sorted({m[3:] for m in MESSAGES + QUERIES}))


def dot(a, b, dims):
    return lax.dot_general(a, b, (dims, ((), ())), preferred_element_type=jnp.float32)


def table(values, index):
    out = values[0]
    for k, v in enumerate(values):
        if k:
            out = jnp.where(index == k, v, out)
    return out


def kernel(
    ring, q_in, nk_in, nv_in, k_hbm, v_hbm, owner_in, hist_in, out,
    qbuf, owner, hist, nk, nv, k_in, v_in, kg, vt, vtn, s0, s1, po, ps, ro, rs,
    l_sem, q_send, q_recv, p_send, p_recv,
):
    here, width = q_in.shape
    heads = width // HD // 2
    rows = here * heads
    hist_rows = kg.shape[1]
    per_req = hist_rows // BLOCK
    blocks = per_req * REQS
    me = lax.axis_index("ctx")
    z, x = lax.div(me, 2), lax.rem(me, 2)

    def device(steps, cross):
        column = 1 - x if cross else x
        return {"ctx": lax.rem(z + (ring + steps) % ring, ring) * 2 + column}

    loads = [
        (q_in.at[:, pl.ds((g * heads + h) * HD, HD)], qbuf.at[0, g, OWN, pl.ds(h * here, here)])
        for g in (A, B)
        for h in range(heads)
    ]
    own_queries = len(loads)
    loads += [(owner_in, owner), (hist_in, hist)]
    loads += [(k_hbm, k_in), (v_hbm, v_in), (nk_in, nk), (nv_in, nv)]
    loads = [pltpu.make_async_copy(a, b, l_sem.at[i]) for i, (a, b) in enumerate(loads)]
    for load in loads:
        load.start()
    barrier = pltpu.get_barrier_semaphore()
    for partner in PARTNERS:
        pl.semaphore_signal(barrier, inc=1, device_id=device(*partner), device_id_type=MESH)
    for load in loads[:own_queries]:
        load.wait()
    pl.semaphore_wait(barrier, len(PARTNERS))

    def q_copy(n):
        p, g, c, steps, cross = QUERIES[n]
        d = (p - steps) % ring
        e = OTH if cross else c
        return pltpu.make_async_remote_copy(
            src_ref=qbuf.at[p, g, c],
            dst_ref=qbuf.at[d, g, e],
            send_sem=q_send.at[n],
            recv_sem=q_recv.at[d, g, e],
            device_id=device(steps, cross),
            device_id_type=MESH,
        )

    def q_wait(p, g, c):
        pltpu.make_async_remote_copy(
            src_ref=qbuf.at[p, g, c],
            dst_ref=qbuf.at[p, g, c],
            send_sem=q_send.at[0],
            recv_sem=q_recv.at[p, g, c],
            device_id=device(*PARTNERS[0]),
            device_id_type=MESH,
        ).wait_recv()

    def p_copies(n):
        p, g, c, steps, cross = MESSAGES[n]
        return [
            pltpu.make_async_remote_copy(
                src_ref=src.at[p, g, c],
                dst_ref=dst.at[n],
                send_sem=p_send.at[n, k],
                recv_sem=p_recv.at[n, k],
                device_id=device(steps, cross),
                device_id_type=MESH,
            )
            for k, (src, dst) in enumerate(((po, ro), (ps, rs)))
        ]

    def merged(parts):
        tops = [s[...] for _, s in parts]
        peak = functools.reduce(jnp.maximum, tops)
        weights = [jnp.exp2(t - peak) for t in tops]
        total = sum(weights[1:], weights[0])
        share = 1.0 / total
        acc = None
        for (o, _), w in zip(parts, weights):
            term = o[...].astype(jnp.float32) * (w * share)
            acc = term if acc is None else acc + term
        return acc, peak + jnp.log(total) * LOG2E

    def take(p, g, c, messages, start=None):
        parts = [start or (po.at[p, g, c], ps.at[p, g, c])]
        for message in messages:
            n = MESSAGES.index(message)
            for copy in p_copies(n):
                copy.wait_recv()
            parts.append((ro.at[n], rs.at[n]))
        return merged(parts)

    def finish(g):
        late = [m for m in LAST[g] if abs(m[3]) > 1]
        acc, lse = take(0, g, OWN, [m for m in LAST[g] if m not in late])
        if late:
            acc, _ = take(0, g, OWN, late, (acc, lse))
        for h in range(heads):
            out[:, pl.ds((g * heads + h) * HD, HD)] = acc[:, h * here : (h + 1) * here].T

    def act(event):
        kind, *rest = event
        if kind == Q:
            q_copy(QUERIES.index(tuple(rest))).start()
        elif kind == S:
            for copy in p_copies(MESSAGES.index(tuple(rest))):
                copy.start()
        elif kind == F:
            p, g, c, messages = rest
            acc, lse = take(p, g, c, messages)
            po[p, g, c] = acc.astype(po.dtype)
            ps[p, g, c] = lse
        else:
            q_wait(*rest)

    arrived = {(0, A, OWN), (0, B, OWN)}

    def with_waits(events, unit):
        result = []
        needs = [(e, [e[1:4]] if e[0] == Q else []) for e in events]
        if unit < len(ORDER):
            needs.append((None, [ORDER[unit] + (c,) for c in (OWN, OTH)]))
        for event, blocks_of in needs:
            for block in blocks_of:
                if block not in arrived:
                    arrived.add(block)
                    result.append((None,) + block)
            if event is not None:
                result.append(event)
        return result

    none = len(ORDER)
    before = [with_waits(es, none) for es in BEFORE[:-2]]
    before += [with_waits(BEFORE[-2], 0), with_waits(BEFORE[-1], 1)]
    after = [with_waits(es, i + 2) for i, es in enumerate(AFTER)]

    for event in before[0]:
        act(event)
    for load in loads[own_queries:]:
        load.wait()

    lane = lax.broadcasted_iota(jnp.int32, (ONES, BLOCK), 1)
    sub = lax.broadcasted_iota(jnp.int32, (BLOCK, HD), 0)
    parts = len(before) - 3
    for i in range(blocks):
        r, b = i // per_req, i % per_req
        at, base = 0, 0
        for j in range(blocks):
            found = lax.div(owner[j], 2 * ring) == i
            at = jnp.where(found, j, at)
            base = jnp.where(found, owner[j], base)
        base = lax.rem(base, per_req * 2 * ring) * BLOCK
        keys = k_in[at]
        vals = v_in[at]
        if b == 0:
            first = keys
        left_over = hist[r] - base
        seen = sub < left_over
        kg[r, pl.ds(b * BLOCK, BLOCK), :] = jnp.where(seen, keys, first)
        vals = jnp.where(seen, vals, jnp.zeros_like(vals))
        vt[r, pl.ds(0, HD), pl.ds(b * BLOCK, BLOCK)] = vals.T
        vt[r, pl.ds(HD, ONES), pl.ds(b * BLOCK, BLOCK)] = jnp.where(
            lane < left_over, 1.0, 0.0
        ).astype(vt.dtype)
        if (i + 1) * parts % blocks == 0:
            for event in before[(i + 1) * parts // blocks]:
                act(event)
    vtn[pl.ds(0, HD), :] = nv[...].T
    vtn[pl.ds(HD, ONES), :] = jnp.ones((ONES, here), vtn.dtype)
    for event in before[-2]:
        act(event)

    step_p = [p for p, _ in ORDER]
    step_g = [g for _, g in ORDER]
    key_row = lax.broadcasted_iota(jnp.int32, (here, 2 * rows), 0)
    col = lax.broadcasted_iota(jnp.int32, (1, 2 * rows), 1)

    def place(i):
        if isinstance(i, int):
            return step_p[i], step_g[i]
        return table(step_p, i), table(step_g, i)

    def request_of(p):
        return lax.div(lax.rem(z + p, ring) * REQS, ring)

    def score(i, s):
        p, g = place(i)
        home = lax.rem(z + p, ring)
        r = request_of(p)
        q = qbuf[p, g].reshape(2 * rows, HD)
        s[pl.ds(0, hist_rows), :] = dot(kg[r], q, ((1,), (1,)))
        fresh = dot(nk[...], q, ((1,), (1,)))
        same = r == lax.div(z * REQS, ring)
        own_tok = jnp.where(same, (home * 2 + x) * here, -here)
        oth_tok = jnp.where(same, (home * 2 + 1 - x) * here, -here)
        query = jnp.where(col < rows, own_tok, oth_tok) + lax.rem(col, here)
        s[pl.ds(hist_rows, here), :] = jnp.where(me * here + key_row <= query, fresh, -1e30)

    def absorb(i, s):
        p, g = place(i)
        r = request_of(p)
        top = jnp.max(s[...], axis=0, keepdims=True) * SCALE
        probs = jnp.exp2(s[pl.ds(0, hist_rows), :] * SCALE - top).astype(jnp.bfloat16)
        fresh = jnp.exp2(s[pl.ds(hist_rows, here), :] * SCALE - top).astype(jnp.bfloat16)
        acc = dot(vt[r], probs, ((1,), (0,))) + dot(vtn[...], fresh, ((1,), (0,)))
        total = acc[HD : HD + 1]
        part = (acc[:HD] * (1.0 / total)).astype(po.dtype)
        lse = top + jnp.log(total) * LOG2E
        for c in (OWN, OTH):
            po[p, g, c] = part[:, c * rows : (c + 1) * rows]
            ps[p, g, c] = lse[:, c * rows : (c + 1) * rows]

    def react(h, half):
        for k in range(len(ORDER) // 2 - 1):
            if after[2 * k + half]:

                @pl.when(h == k)
                def _():
                    for event in after[2 * k + half]:
                        act(event)

    score(0, s0)
    for event in before[-1]:
        act(event)

    @pl.loop(0, len(ORDER) // 2 - 1)
    def _(h):
        score(2 * h + 1, s1)
        absorb(2 * h, s0)
        react(h, 0)
        score(2 * h + 2, s0)
        absorb(2 * h + 1, s1)
        react(h, 1)

    last = len(ORDER) - 1
    score(last, s1)
    absorb(last - 1, s0)
    for event in after[last - 1]:
        act(event)
    absorb(last, s1)
    for event in after[last] + after[last + 1]:
        act(event)
    for n in range(len(QUERIES)):
        q_copy(n).wait_send()
    for n in range(len(MESSAGES)):
        for copy in p_copies(n):
            copy.wait_send()
    finish(A)
    finish(B)


def local(queries, new_keys, new_values, cache_keys, cache_values, block_owner, history_len):
    here, width = queries.shape
    ring = lax.axis_size("ctx") // 2
    heads = width // HD
    rows = here * heads // 2
    slots = cache_keys.shape[0]
    hist_rows = slots // REQS
    bf, f32 = jnp.bfloat16, jnp.float32
    hbm = pl.BlockSpec(memory_space=pltpu.HBM)
    dma = pltpu.SemaphoreType.DMA
    all_rows = 4 * rows * ring
    keys = hist_rows + here
    return pl.pallas_call(
        functools.partial(kernel, ring),
        out_shape=pltpu.VMEM((here, width), f32),
        in_specs=[hbm] * 7,
        out_specs=pl.BlockSpec(memory_space=pltpu.VMEM),
        scratch_shapes=[
            pltpu.VMEM((ring, 2, 2, rows, HD), bf),
            pltpu.SMEM(block_owner.shape, jnp.int32),
            pltpu.SMEM(history_len.shape, jnp.int32),
            pltpu.VMEM((here, HD), bf),
            pltpu.VMEM((here, HD), bf),
            pltpu.VMEM((slots // BLOCK, BLOCK, HD), bf),
            pltpu.VMEM((slots // BLOCK, BLOCK, HD), bf),
            pltpu.VMEM((REQS, hist_rows, HD), bf),
            pltpu.VMEM((REQS, HD + ONES, hist_rows), bf),
            pltpu.VMEM((HD + ONES, here), bf),
            pltpu.VMEM((keys, 2 * rows), f32),
            pltpu.VMEM((keys, 2 * rows), f32),
            pltpu.VMEM((ring, 2, 2, HD, rows), bf),
            pltpu.VMEM((ring, 2, 2, 1, rows), f32),
            pltpu.VMEM((len(MESSAGES), HD, rows), bf),
            pltpu.VMEM((len(MESSAGES), 1, rows), f32),
            dma((heads + 6,)),
            dma((len(QUERIES),)),
            dma((ring, 2, 2)),
            dma((len(MESSAGES), 2)),
            dma((len(MESSAGES), 2)),
        ],
        compiler_params=pltpu.CompilerParams(
            collective_id=0, has_side_effects=True, vmem_limit_bytes=54 * 2**20
        ),
        cost_estimate=pl.CostEstimate(
            flops=4 * all_rows * keys * HD,
            bytes_accessed=4 * slots * HD + 6 * here * width,
            transcendentals=all_rows * keys,
        ),
    )(
        queries,
        new_keys,
        new_values,
        cache_keys.reshape(-1, BLOCK, HD),
        cache_values.reshape(-1, BLOCK, HD),
        block_owner,
        history_len,
    )


def solution(mesh):
    rows = P(("rep", "ctx"), "tp")
    return jax.shard_map(
        local,
        mesh=mesh,
        in_specs=(rows,) * 5 + (P(("rep", "ctx")), P("rep")),
        out_specs=rows,
        check_vma=False,
    )
```

```python
import functools
import math

import jax
import jax.numpy as jnp
from jax import lax
from jax.experimental import pallas as pl
from jax.experimental.pallas import tpu as pltpu
from jax.sharding import PartitionSpec as P

HD = 128
REQS = 2
BLOCK = 256
LOG2E = math.log2(math.e)
SCALE = LOG2E / math.sqrt(HD)
MESH = pl.DeviceIdType.MESH
A, B = 0, 1
OWN, OTH = 0, 1
ONES = 16
Q, S, F = 0, 1, 2

ORDER = (
    (7, 0),
    (0, 0),
    (1, 0),
    (1, 1),
    (6, 0),
    (2, 0),
    (7, 1),
    (5, 0),
    (3, 0),
    (3, 1),
    (4, 0),
    (4, 1),
    (5, 1),
    (6, 1),
    (2, 1),
    (0, 1),
)
BEFORE = (
    ((Q, 0, 0, 0, 1, 1), (Q, 0, 1, 0, -1, 0), (Q, 0, 0, 0, 1, 0), (Q, 0, 1, 0, 1, 0), (Q, 0, 0, 0, -1, 0), (Q, 0, 0, 0, 0, 1), (Q, 0, 0, 0, -1, 1), (Q, 0, 1, 0, 0, 1),),
    (),
    (),
    (),
    (),
    (),
    (),
    (),
    (),
    ((Q, 1, 1, 0, 0, 1), (Q, 1, 1, 0, -1, 0), (Q, 7, 0, 1, 1, 0), (Q, 7, 0, 0, 1, 0), (Q, 1, 0, 0, -1, 0),),
    (),
)
AFTER = (
    ((Q, 7, 1, 0, 1, 0), (Q, 1, 0, 1, -1, 0), (Q, 7, 1, 0, 0, 1),),
    ((Q, 2, 1, 0, -1, 0), (Q, 6, 0, 1, 1, 0), (Q, 2, 1, 0, 0, 1), (S, 0, 0, 1, 0, 1),),
    ((Q, 6, 0, 0, 1, 0), (Q, 2, 0, 0, -1, 0),),
    ((Q, 6, 1, 0, 0, 1), (Q, 2, 0, 1, -1, 0), (Q, 6, 1, 0, 1, 0), (S, 1, 1, 1, 0, 1),),
    ((Q, 3, 1, 0, 0, 1), (Q, 5, 0, 1, 1, 0), (Q, 3, 1, 0, -1, 1), (Q, 3, 1, 0, -1, 0),),
    ((Q, 5, 0, 0, 1, 0),),
    ((Q, 5, 1, 0, 0, 1), (S, 7, 1, 1, 0, 1),),
    ((S, 5, 0, 0, -1, 0), (S, 5, 0, 1, -1, 0), (F, 1, 1, 0, ((1, 1, 1, 0, 1),)), (S, 1, 1, 0, 1, 0),),
    ((S, 3, 0, 0, 1, 0), (S, 3, 0, 1, 1, 0),),
    ((S, 3, 1, 1, 0, 1),),
    ((S, 4, 0, 1, 2, 0), (S, 4, 0, 0, -2, 0), (F, 7, 1, 0, ((7, 1, 1, 0, 1),)), (S, 7, 1, 0, -1, 0),),
    ((S, 4, 1, 1, 0, 1), (F, 2, 0, 0, ((3, 0, 0, 1, 0),)), (S, 2, 0, 0, 1, 0), (F, 6, 0, 1, ((5, 0, 1, -1, 0),)), (S, 6, 0, 1, -1, 0),),
    ((S, 5, 1, 1, 0, 1), (F, 3, 1, 0, ((3, 1, 1, 0, 1),)), (S, 3, 1, 0, 1, 0),),
    ((F, 6, 0, 0, ((4, 0, 0, -2, 0), (5, 0, 0, -1, 0))), (S, 6, 0, 0, -1, 0), (S, 6, 1, 1, 0, 1), (F, 2, 0, 1, ((4, 0, 1, 2, 0), (3, 0, 1, 1, 0))), (S, 2, 0, 1, 1, 0),),
    ((F, 4, 1, 0, ((4, 1, 1, 0, 1),)), (S, 4, 1, 0, 2, 0), (S, 2, 1, 1, 0, 1), (F, 1, 0, 0, ((2, 0, 0, 1, 0),)), (S, 1, 0, 0, 1, 0),),
    ((F, 5, 1, 0, ((5, 1, 1, 0, 1),)), (S, 5, 1, 0, -1, 0), (S, 0, 1, 1, 0, 1), (F, 7, 0, 1, ((6, 0, 1, -1, 0),)), (S, 7, 0, 1, -1, 1),),
    ((F, 6, 1, 0, ((6, 1, 1, 0, 1),)), (F, 1, 0, 1, ((2, 0, 1, 1, 0),)), (S, 1, 0, 1, 1, 1), (F, 7, 0, 0, ((6, 0, 0, -1, 0),)), (S, 7, 0, 0, -1, 0), (F, 2, 1, 0, ((2, 1, 1, 0, 1),)), (F, 2, 1, 0, ((4, 1, 0, 2, 0), (3, 1, 0, 1, 0))), (S, 2, 1, 0, 2, 0), (F, 6, 1, 0, ((5, 1, 0, -1, 0),)), (S, 6, 1, 0, -2, 0),),
)
LAST = (
    ((1, 0, 0, 1, 0), (7, 0, 0, -1, 0), (1, 0, 1, 1, 1), (7, 0, 1, -1, 1), (0, 0, 1, 0, 1),),
    ((2, 1, 0, 2, 0), (1, 1, 0, 1, 0), (6, 1, 0, -2, 0), (7, 1, 0, -1, 0), (0, 1, 1, 0, 1),),
)

MESSAGES = tuple(e[1:] for es in BEFORE + AFTER for e in es if e[0] == S)
QUERIES = tuple(e[1:] for es in BEFORE + AFTER for e in es if e[0] == Q)
PARTNERS = tuple(sorted({m[3:] for m in MESSAGES + QUERIES}))


def dot(a, b, dims):
    return lax.dot_general(a, b, (dims, ((), ())), preferred_element_type=jnp.float32)


def table(values, index):
    out = values[0]
    for k, v in enumerate(values):
        if k:
            out = jnp.where(index == k, v, out)
    return out


def kernel(
    ring, q_in, nk_in, nv_in, k_hbm, v_hbm, owner_in, hist_in, out,
    qbuf, owner, hist, nk, nv, k_in, v_in, kg, vt, vtn, s0, s1, po, ps, ro, rs,
    l_sem, q_send, q_recv, p_send, p_recv,
):
    here, width = q_in.shape
    heads = width // HD // 2
    rows = here * heads
    hist_rows = kg.shape[1]
    per_req = hist_rows // BLOCK
    blocks = per_req * REQS
    me = lax.axis_index("ctx")
    z, x = lax.div(me, 2), lax.rem(me, 2)

    def device(steps, cross):
        column = 1 - x if cross else x
        return {"ctx": lax.rem(z + (ring + steps) % ring, ring) * 2 + column}

    loads = [
        (q_in.at[:, pl.ds((g * heads + h) * HD, HD)], qbuf.at[0, g, OWN, pl.ds(h * here, here)])
        for g in (A, B)
        for h in range(heads)
    ]
    own_queries = len(loads)
    loads += [(owner_in, owner), (hist_in, hist)]
    loads += [(k_hbm, k_in), (v_hbm, v_in), (nk_in, nk), (nv_in, nv)]
    loads = [pltpu.make_async_copy(a, b, l_sem.at[i]) for i, (a, b) in enumerate(loads)]
    for load in loads:
        load.start()
    barrier = pltpu.get_barrier_semaphore()
    for partner in PARTNERS:
        pl.semaphore_signal(barrier, inc=1, device_id=device(*partner), device_id_type=MESH)
    for load in loads[:own_queries]:
        load.wait()
    pl.semaphore_wait(barrier, len(PARTNERS))

    def q_copy(n):
        p, g, c, steps, cross = QUERIES[n]
        d = (p - steps) % ring
        e = OTH if cross else c
        return pltpu.make_async_remote_copy(
            src_ref=qbuf.at[p, g, c],
            dst_ref=qbuf.at[d, g, e],
            send_sem=q_send.at[n],
            recv_sem=q_recv.at[d, g, e],
            device_id=device(steps, cross),
            device_id_type=MESH,
        )

    def q_wait(p, g, c):
        pltpu.make_async_remote_copy(
            src_ref=qbuf.at[p, g, c],
            dst_ref=qbuf.at[p, g, c],
            send_sem=q_send.at[0],
            recv_sem=q_recv.at[p, g, c],
            device_id=device(*PARTNERS[0]),
            device_id_type=MESH,
        ).wait_recv()

    def p_copies(n):
        p, g, c, steps, cross = MESSAGES[n]
        return [
            pltpu.make_async_remote_copy(
                src_ref=src.at[p, g, c],
                dst_ref=dst.at[n],
                send_sem=p_send.at[n, k],
                recv_sem=p_recv.at[n, k],
                device_id=device(steps, cross),
                device_id_type=MESH,
            )
            for k, (src, dst) in enumerate(((po, ro), (ps, rs)))
        ]

    def merged(parts):
        tops = [s[...] for _, s in parts]
        peak = functools.reduce(jnp.maximum, tops)
        weights = [jnp.exp2(t - peak) for t in tops]
        total = sum(weights[1:], weights[0])
        share = 1.0 / total
        acc = None
        for (o, _), w in zip(parts, weights):
            term = o[...].astype(jnp.float32) * (w * share)
            acc = term if acc is None else acc + term
        return acc, peak + jnp.log(total) * LOG2E

    def take(p, g, c, messages):
        parts = [(po.at[p, g, c], ps.at[p, g, c])]
        for message in messages:
            n = MESSAGES.index(message)
            for copy in p_copies(n):
                copy.wait_recv()
            parts.append((ro.at[n], rs.at[n]))
        return merged(parts)

    def finish(g):
        acc, _ = take(0, g, OWN, LAST[g])
        for h in range(heads):
            out[:, pl.ds((g * heads + h) * HD, HD)] = acc[:, h * here : (h + 1) * here].T

    def act(event):
        kind, *rest = event
        if kind == Q:
            q_copy(QUERIES.index(tuple(rest))).start()
        elif kind == S:
            for copy in p_copies(MESSAGES.index(tuple(rest))):
                copy.start()
        elif kind == F:
            p, g, c, messages = rest
            acc, lse = take(p, g, c, messages)
            po[p, g, c] = acc.astype(po.dtype)
            ps[p, g, c] = lse
        else:
            q_wait(*rest)

    arrived = {(0, A, OWN), (0, B, OWN)}

    def with_waits(events, unit):
        result = []
        needs = [(e, [e[1:4]] if e[0] == Q else []) for e in events]
        if unit < len(ORDER):
            needs.append((None, [ORDER[unit] + (c,) for c in (OWN, OTH)]))
        for event, blocks_of in needs:
            for block in blocks_of:
                if block not in arrived:
                    arrived.add(block)
                    result.append((None,) + block)
            if event is not None:
                result.append(event)
        return result

    none = len(ORDER)
    before = [with_waits(es, none) for es in BEFORE[:-2]]
    before += [with_waits(BEFORE[-2], 0), with_waits(BEFORE[-1], 1)]
    after = [with_waits(es, i + 2) for i, es in enumerate(AFTER)]

    for event in before[0]:
        act(event)
    for load in loads[own_queries:]:
        load.wait()

    lane = lax.broadcasted_iota(jnp.int32, (ONES, BLOCK), 1)
    sub = lax.broadcasted_iota(jnp.int32, (BLOCK, HD), 0)
    parts = len(before) - 3
    for i in range(blocks):
        r, b = i // per_req, i % per_req
        at, base = 0, 0
        for j in range(blocks):
            found = lax.div(owner[j], 2 * ring) == i
            at = jnp.where(found, j, at)
            base = jnp.where(found, owner[j], base)
        base = lax.rem(base, per_req * 2 * ring) * BLOCK
        keys = k_in[at]
        vals = v_in[at]
        if b == 0:
            first = keys
        left_over = hist[r] - base
        seen = sub < left_over
        kg[r, pl.ds(b * BLOCK, BLOCK), :] = jnp.where(seen, keys, first)
        vals = jnp.where(seen, vals, jnp.zeros_like(vals))
        vt[r, pl.ds(0, HD), pl.ds(b * BLOCK, BLOCK)] = vals.T
        vt[r, pl.ds(HD, ONES), pl.ds(b * BLOCK, BLOCK)] = jnp.where(
            lane < left_over, 1.0, 0.0
        ).astype(vt.dtype)
        if (i + 1) * parts % blocks == 0:
            for event in before[(i + 1) * parts // blocks]:
                act(event)
    vtn[pl.ds(0, HD), :] = nv[...].T
    vtn[pl.ds(HD, ONES), :] = jnp.ones((ONES, here), vtn.dtype)
    for event in before[-2]:
        act(event)

    step_p = [p for p, _ in ORDER]
    step_g = [g for _, g in ORDER]
    key_row = lax.broadcasted_iota(jnp.int32, (here, 2 * rows), 0)
    col = lax.broadcasted_iota(jnp.int32, (1, 2 * rows), 1)

    def place(i):
        if isinstance(i, int):
            return step_p[i], step_g[i]
        return table(step_p, i), table(step_g, i)

    def request_of(p):
        return lax.div(lax.rem(z + p, ring) * REQS, ring)

    def score(i, s):
        p, g = place(i)
        home = lax.rem(z + p, ring)
        r = request_of(p)
        q = qbuf[p, g].reshape(2 * rows, HD)
        s[pl.ds(0, hist_rows), :] = dot(kg[r], q, ((1,), (1,)))
        fresh = dot(nk[...], q, ((1,), (1,)))
        same = r == lax.div(z * REQS, ring)
        own_tok = jnp.where(same, (home * 2 + x) * here, -here)
        oth_tok = jnp.where(same, (home * 2 + 1 - x) * here, -here)
        query = jnp.where(col < rows, own_tok, oth_tok) + lax.rem(col, here)
        s[pl.ds(hist_rows, here), :] = jnp.where(me * here + key_row <= query, fresh, -1e30)

    def absorb(i, s):
        p, g = place(i)
        r = request_of(p)
        top = jnp.max(s[...], axis=0, keepdims=True) * SCALE
        probs = jnp.exp2(s[pl.ds(0, hist_rows), :] * SCALE - top).astype(jnp.bfloat16)
        fresh = jnp.exp2(s[pl.ds(hist_rows, here), :] * SCALE - top).astype(jnp.bfloat16)
        acc = dot(vt[r], probs, ((1,), (0,))) + dot(vtn[...], fresh, ((1,), (0,)))
        total = acc[HD : HD + 1]
        part = (acc[:HD] * (1.0 / total)).astype(po.dtype)
        lse = top + jnp.log(total) * LOG2E
        for c in (OWN, OTH):
            po[p, g, c] = part[:, c * rows : (c + 1) * rows]
            ps[p, g, c] = lse[:, c * rows : (c + 1) * rows]

    def react(h, half):
        for k in range(len(ORDER) // 2 - 1):
            if after[2 * k + half]:

                @pl.when(h == k)
                def _():
                    for event in after[2 * k + half]:
                        act(event)

    score(0, s0)
    for event in before[-1]:
        act(event)

    @pl.loop(0, len(ORDER) // 2 - 1)
    def _(h):
        score(2 * h + 1, s1)
        absorb(2 * h, s0)
        react(h, 0)
        score(2 * h + 2, s0)
        absorb(2 * h + 1, s1)
        react(h, 1)

    last = len(ORDER) - 1
    score(last, s1)
    absorb(last - 1, s0)
    for event in after[last - 1]:
        act(event)
    absorb(last, s1)
    for event in after[last] + after[last + 1]:
        act(event)
    for n in range(len(QUERIES)):
        q_copy(n).wait_send()
    for n in range(len(MESSAGES)):
        for copy in p_copies(n):
            copy.wait_send()
    finish(A)
    finish(B)


def local(queries, new_keys, new_values, cache_keys, cache_values, block_owner, history_len):
    here, width = queries.shape
    ring = lax.axis_size("ctx") // 2
    heads = width // HD
    rows = here * heads // 2
    slots = cache_keys.shape[0]
    hist_rows = slots // REQS
    bf, f32 = jnp.bfloat16, jnp.float32
    hbm = pl.BlockSpec(memory_space=pltpu.HBM)
    dma = pltpu.SemaphoreType.DMA
    all_rows = 4 * rows * ring
    keys = hist_rows + here
    return pl.pallas_call(
        functools.partial(kernel, ring),
        out_shape=pltpu.VMEM((here, width), f32),
        in_specs=[hbm] * 7,
        out_specs=pl.BlockSpec(memory_space=pltpu.VMEM),
        scratch_shapes=[
            pltpu.VMEM((ring, 2, 2, rows, HD), bf),
            pltpu.SMEM(block_owner.shape, jnp.int32),
            pltpu.SMEM(history_len.shape, jnp.int32),
            pltpu.VMEM((here, HD), bf),
            pltpu.VMEM((here, HD), bf),
            pltpu.VMEM((slots // BLOCK, BLOCK, HD), bf),
            pltpu.VMEM((slots // BLOCK, BLOCK, HD), bf),
            pltpu.VMEM((REQS, hist_rows, HD), bf),
            pltpu.VMEM((REQS, HD + ONES, hist_rows), bf),
            pltpu.VMEM((HD + ONES, here), bf),
            pltpu.VMEM((keys, 2 * rows), f32),
            pltpu.VMEM((keys, 2 * rows), f32),
            pltpu.VMEM((ring, 2, 2, HD, rows), bf),
            pltpu.VMEM((ring, 2, 2, 1, rows), f32),
            pltpu.VMEM((len(MESSAGES), HD, rows), bf),
            pltpu.VMEM((len(MESSAGES), 1, rows), f32),
            dma((heads + 6,)),
            dma((len(QUERIES),)),
            dma((ring, 2, 2)),
            dma((len(MESSAGES), 2)),
            dma((len(MESSAGES), 2)),
        ],
        compiler_params=pltpu.CompilerParams(
            collective_id=0, has_side_effects=True, vmem_limit_bytes=54 * 2**20
        ),
        cost_estimate=pl.CostEstimate(
            flops=4 * all_rows * keys * HD,
            bytes_accessed=4 * slots * HD + 6 * here * width,
            transcendentals=all_rows * keys,
        ),
    )(
        queries,
        new_keys,
        new_values,
        cache_keys.reshape(-1, BLOCK, HD),
        cache_values.reshape(-1, BLOCK, HD),
        block_owner,
        history_len,
    )


def solution(mesh):
    rows = P(("rep", "ctx"), "tp")
    return jax.shard_map(
        local,
        mesh=mesh,
        in_specs=(rows,) * 5 + (P(("rep", "ctx")), P("rep")),
        out_specs=rows,
        check_vma=False,
    )
```
